512 devices in a mesh: section: 16 (over x_hi, z), tp: 32 (over y, x_lo, core).
Axes of the slice: x: 4 (x_hi: 2, x_lo: 2; x = x_hi * 2 + x_lo), y: 8, z: 8, core: 2. Of those that a mesh axis runs over, the one named last changes fastest.
Arguments:
- resid: bfloat16 [512, 4608], P('tp', 'section'), may hold values from -40 to 40
- act: bfloat16 [512, 36864], P(None, 'tp'), may hold values from -6 to 6
- w_down: bfloat16 [36864, 4608], P('tp', 'section'), may hold values from -0.03125 to 0.03125
- gain: float32 [4608], P('section'), may hold values from 0.1 to 1.9
- embed: bfloat16 [4608, 131072], P(None, ('section', 'tp')), may hold values from -24 to 24
- targets: int32 [512], replicated, may hold values from 0 to 131071
Outputs:
- final_hidden: bfloat16 [512, 4608], P('tp', 'section')
- logprob: float32 [512], replicated
The draws below stay inside these ranges and needn't reach their ends.
All inputs are finite; a program needn't handle non-finite values.
Results may differ from the reference program's by a relative error of at most 0.0014.
Values may be sent and summed in bfloat16 or wider, within the bound.
A program may use at most 64 MiB of HBM per device.

```python
import jax
import jax.numpy as jnp
from jax import lax

D = 4608
FF = 36864
ROWS = 512
VOCAB = 131072
N_SECTION = 16


def shared_rows(key):
    return jnp.clip(jax.random.normal(jax.random.fold_in(key, 99), (4, D), jnp.float32), -4.0, 4.0)


def draw_resid(key, part):
    shared = shared_rows(key)
    key = jax.random.fold_in(key, 11)
    first = jax.random.fold_in(key, 0)
    base = jnp.clip(jax.random.normal(first, (ROWS, D), jnp.float32), -6.0, 6.0)
    places = jnp.arange(4) * (ROWS // 4) + ROWS // 8
    base = base.at[places].set(8.0 * shared)
    return base.astype(jnp.bfloat16)


def draw_embed(key, part):
    shared = shared_rows(key)
    key = jax.random.fold_in(key, 12)
    first = jax.random.fold_in(key, 0)
    base = jnp.clip(jax.random.normal(first, (D, VOCAB), jnp.float32), -6.0, 6.0) * (3.0 / jnp.sqrt(D * 1.0))
    strengths = jnp.array([1.2, 2.0, 2.8, 3.6], jnp.float32)
    places = jnp.arange(4) * (VOCAB // 4) + 5
    norm_scale = 100.0 / (D * 1.0)
    base = base.at[:, places].set((strengths[:, None] * shared).T * norm_scale)
    base = base.at[:, places + VOCAB // 8].set(((strengths + 0.015)[:, None] * shared).T * norm_scale)
    return base.astype(jnp.bfloat16)


def plant(entries, rng, smallest, high):
    extent = entries.shape
    place = [jax.random.randint(jax.random.fold_in(rng, axis), (), 0, extent[axis]) for axis in range(len(extent))]
    entries = entries.at[tuple(place)].set(smallest)
    longest = extent.index(max(extent))
    place[longest] = (place[longest] + 1) % extent[longest]
    return entries.at[tuple(place)].set(high)


def shard_levels(stream_key, extent, shards, low, top_value):
    level = 1.0
    for axis_at, parts in shards:
        draws = jax.random.uniform(jax.random.fold_in(jax.random.fold_in(stream_key, 6), axis_at), (parts,), jnp.float32, low / len(shards), top_value / len(shards))
        level = level * jnp.repeat(jnp.exp(draws), extent[axis_at] // parts).reshape((-1,) + (1,) * (len(extent) - 1 - axis_at))
    return level


def normal_values(rng, shape, deviation, most, pieces=(), kind=jnp.bfloat16):
    result = deviation * jax.random.normal(rng, shape, jnp.float32)
    if pieces:
        result = result * shard_levels(rng, shape, pieces, -0.22, 0.18)
    return jnp.clip(result, -most, most).astype(kind)


def setup_inputs(seed: int = 0) -> dict:
    arg_keys = jax.random.split(jax.random.key(seed), 7)
    return {
        "resid": draw_resid(jax.random.fold_in(arg_keys[6], 71), 0),
        "act": normal_values(arg_keys[1], (ROWS, FF), 1.0, 6.0, ((1, 32),)),
        "w_down": normal_values(arg_keys[2], (FF, D), FF ** -0.5, 0.03125, ((0, 32), (1, 16))),
        "gain": jnp.clip(1.0 + 0.18 * jax.random.normal(arg_keys[3], (D,), jnp.float32), 0.1, 1.9),
        "embed": draw_embed(jax.random.fold_in(arg_keys[6], 71), 0),
        "targets": plant(jax.random.randint(arg_keys[5], (ROWS,), 0, VOCAB), jax.random.fold_in(arg_keys[5], 1), 0, VOCAB - 1).astype(jnp.int32),
    }


def reference(resid, act, w_down, gain, embed, targets):
    mixed = resid.astype(jnp.float32) + jnp.dot(act, w_down, preferred_element_type=jnp.float32)
    mean_sq = lax.optimization_barrier(jnp.mean(mixed * mixed, axis=1))
    final_hidden = (mixed * lax.rsqrt(mean_sq + 1e-06)[:, None] * gain[None, :]).astype(jnp.bfloat16)
    width = VOCAB // N_SECTION

    def step(index, carry):
        top, total, target_logit = carry
        start = (index * width).astype(jnp.int32)
        columns = lax.dynamic_slice_in_dim(embed, start, width, 1)
        logits = jnp.dot(final_hidden, columns, preferred_element_type=jnp.float32)
        block_top = lax.optimization_barrier(jnp.max(logits, axis=1))
        new_top = jnp.maximum(top, block_top)
        total = total * jnp.exp(top - new_top) + lax.optimization_barrier(jnp.sum(jnp.exp(logits - new_top[:, None]), axis=1))
        places = jnp.arange(width, dtype=jnp.int32)[None, :] + start
        chosen = places == targets[:, None]
        target_logit = target_logit + lax.optimization_barrier(jnp.sum(jnp.where(chosen, logits, jnp.zeros_like(logits)), axis=1))
        return (new_top, total, target_logit)
    start_top = jnp.full((ROWS,), -1e+30, jnp.float32)
    zeros = jnp.zeros((ROWS,), jnp.float32)
    top, total, target_logit = lax.fori_loop(0, N_SECTION, step, (start_top, zeros, zeros))
    logprob = target_logit - top - jnp.log(total)
    return (final_hidden, logprob)
```

```python
import jax
import jax.numpy as jnp
from jax import lax
from jax.experimental import pallas as pl
from jax.experimental.pallas import tpu as pltpu
from jax.sharding import PartitionSpec as P

MESH = pl.DeviceIdType.MESH
F32 = jnp.float32
BF16 = jnp.bfloat16
HID, WID = 1152, 288
D_ALL = 4608
PADW = 384
COLS = 256


def send(src, dst, s_sem, r_sem, dev):
    return pltpu.make_async_remote_copy(
        src_ref=src, dst_ref=dst, send_sem=s_sem, recv_sem=r_sem, device_id=dev, device_id_type=MESH
    )


def kernel(
    act, w_down, resid, gain, embed, targets,
    fh_out, lp_out,
    a_buf, w_buf, r_in, g_in, t_in, e_buf,
    p_out, p_in, p_own, s_buf, s_in, m_buf, h_buf, scale_buf, acc,
    st1, st2, res,
    ld_sem, core_s, core_r, rs_s, rs_r, pl_s, pl_r, ring_s, ring_r, s1_s, s1_r, s2_s, s2_r,
):
    sec = lax.axis_index("section")
    tp = lax.axis_index("tp")
    core = lax.rem(tp, 2)
    xl = lax.rem(tp // 2, 2)
    y = tp // 4
    xh = sec // 8
    z = lax.rem(sec, 8)
    x = 2 * xh + xl
    first = core == 0
    u = jnp.where(first, y, z)
    w = jnp.where(first, z, y)

    def dev(x2, y2, z2, c2):
        return ((x2 // 2) * 8 + z2, (y2 * 2 + lax.rem(x2, 2)) * 2 + c2)

    sibling = dev(x, y, z, 1 - core)

    def rs_peer(i):
        return lax.rem(y + i // 2, 8), lax.rem(xl + i, 2)

    def rs_dev(i):
        y2, xl2 = rs_peer(i)
        return dev(2 * xh + xl2, y2, z, core)

    def grid_dev(x2, u2, w2):
        return dev(x2, jnp.where(first, u2, w2), jnp.where(first, w2, u2), core)

    def plane_dev(i):
        return grid_dev(lax.rem(x + i // 8, 4), lax.rem(u + i, 8), w)

    def line_dev(i):
        return grid_dev(x, u, lax.rem(w + i, 8))

    def load(src, dst, k):
        return pltpu.make_async_copy(src, dst, ld_sem.at[k])

    l_w = load(w_down, w_buf, 0)
    l_a0 = load(act.at[:, 1 - core], a_buf.at[0], 1)
    l_a1 = load(act.at[:, core], a_buf.at[1], 2)
    l_r = load(resid, r_in, 3)
    l_g = load(gain, g_in, 4)
    l_t = load(targets.at[core], t_in, 5)
    l_e = load(embed, e_buf.at[core, :, pl.ds(0, WID), :], 6)
    for l in (l_w, l_a0, l_a1, l_r, l_g, l_t, l_e):
        l.start()

    barrier = pltpu.get_barrier_semaphore()
    pl.semaphore_signal(barrier, inc=1, device_id=sibling, device_id_type=MESH)

    def sig(peer):
        def go(i, carry):
            pl.semaphore_signal(barrier, inc=1, device_id=peer(i), device_id_type=MESH)
            return carry
        return go

    lax.fori_loop(1, 16, sig(rs_dev), 0)
    lax.fori_loop(1, 32, sig(plane_dev), 0)
    lax.fori_loop(1, 8, sig(line_dev), 0)

    def zero(s, carry):
        for c in range(2):
            e_buf[c, s, pl.ds(WID, PADW - WID), :] = jnp.zeros((PADW - WID, COLS), BF16)
        return carry

    lax.fori_loop(0, 16, zero, 0)
    p_out[:, pl.ds(256, 128)] = jnp.zeros((256, 128), F32)
    p_own[:, pl.ds(256, 128)] = jnp.zeros((256, 128), F32)

    def partial(k):
        return lax.dot_general(
            a_buf[k].reshape(256, HID), w_buf[...], (((1,), (1,)), ((), ())), preferred_element_type=F32
        )

    l_w.wait()
    l_a0.wait()
    p_out[:, pl.ds(0, WID)] = partial(0)
    pl.semaphore_wait(barrier, 1 + 15 + 31 + 7)
    c_pair = send(p_out, p_in, core_s.at[0], core_r.at[0], sibling)
    c_pair.start()
    l_a1.wait()
    p_own[:, pl.ds(0, WID)] = partial(1)
    c_pair.wait_recv()
    for b in range(16):
        rows = pl.ds(16 * b, 16)
        v = p_own[rows, :] + p_in[rows, :]
        s_buf[b, 0] = v[0:8, 0:128]
        s_buf[b, 1] = v[0:8, 128:256]
        s_buf[b, 2] = v[8:16, 0:128]
        s_buf[b, 3] = v[8:16, 128:256]
        s_buf[b, 4] = v[0:8, 256:384] + pltpu.roll(v[8:16, 256:384], 32, 1)

    def rs_copy(i):
        y2, xl2 = rs_peer(i)
        return send(s_buf.at[y2 * 2 + xl2], s_in.at[i], rs_s.at[i], rs_r.at[i], rs_dev(i))

    def rs_start(i, carry):
        rs_copy(i).start()
        return carry

    lax.fori_loop(1, 16, rs_start, 0)

    l_e.wait()
    c_emb = send(
        e_buf.at[core, :, pl.ds(0, WID), :], e_buf.at[core, :, pl.ds(0, WID), :],
        core_s.at[1], core_r.at[1], sibling,
    )
    c_emb.start()
    l_r.wait()
    l_g.wait()
    l_t.wait()

    def rs_wait(i, carry):
        rs_copy(i).wait_recv()
        return carry

    lax.fori_loop(1, 16, rs_wait, 0)
    total = s_buf[y * 2 + xl]
    for i in range(1, 16):
        total = total + s_in[i]
    lane8 = lax.broadcasted_iota(jnp.int32, (8, 128), 1)
    m_buf[0:8, 0:128] = total[0]
    m_buf[0:8, 128:256] = total[1]
    m_buf[8:16, 0:128] = total[2]
    m_buf[8:16, 128:256] = total[3]
    m_buf[0:8, 256:384] = jnp.where(lane8 < 32, total[4], 0.0)
    m_buf[8:16, 256:384] = jnp.where(lane8 < 32, pltpu.roll(total[4], 96, 1), 0.0)
    mixed = m_buf[:, pl.ds(0, WID)] + r_in[...].astype(F32)
    m_buf[:, pl.ds(0, WID)] = mixed
    sq = jnp.sum(mixed * mixed, axis=1, keepdims=True)
    sq_hi = sq.astype(BF16).astype(F32)
    sq_rest = sq - sq_hi
    sq_mid = sq_rest.astype(BF16).astype(F32)
    sq_lo = (sq_rest - sq_mid).astype(BF16).astype(F32)
    m_own = h_buf.at[w, x * 8 + u]
    lane = lax.broadcasted_iota(jnp.int32, (16, 128), 1)
    tail = jnp.where(lane == 32, sq_hi, jnp.where(lane == 33, sq_mid, jnp.where(lane == 34, sq_lo, 0.0)))
    m_own[:, pl.ds(256, 128)] = tail.astype(BF16)
    m_own[:, pl.ds(0, WID)] = (mixed * g_in[...]).astype(BF16)

    def pl_copy(i):
        return send(h_buf.at[w, x * 8 + u], h_buf.at[w, x * 8 + u], pl_s.at[i], pl_r.at[i], plane_dev(i))

    def pl_start(i, carry):
        pl_copy(i).start()
        return carry

    def pl_wait(i, carry):
        pl_copy(i).wait_recv()
        return carry

    lax.fori_loop(1, 32, pl_start, 0)
    lax.fori_loop(1, 32, pl_wait, 0)

    right, left = line_dev(1), line_dev(7)

    def ring_copy(way, k, c):
        at = lax.rem(w + (8 - (k - 1) if way == 0 else k - 1), 8)
        part = h_buf.at[at, pl.ds(16 * c, 16)]
        j = (way * 4 + k - 1) * 2 + c
        return send(part, part, ring_s.at[j], ring_r.at[j], right if way == 0 else left)

    hops = {(0, 0): 4, (0, 1): 3, (1, 0): 3, (1, 1): 4}
    sent = []
    for k in range(1, 6):
        for c in range(2):
            for way in range(2):
                if 2 <= k <= hops[way, c] + 1:
                    ring_copy(way, k - 1, c).wait_recv()
                if k <= hops[way, c]:
                    cp = ring_copy(way, k, c)
                    cp.start()
                    sent.append(cp)
    c_emb.wait_recv()

    sel = (lane >= 32) & (lane < 35)

    def slot(y2, x2, z2):
        return jnp.where(first, z2, y2), x2 * 8 + jnp.where(first, y2, z2)

    def norm(b, carry):
        y2, xl2 = b // 2, lax.rem(b, 2)
        t = jnp.zeros((16, 128), F32)
        for s in range(16):
            w2, p2 = slot(y2, 2 * (s // 8) + xl2, s % 8)
            t = t + h_buf[w2, p2, :, pl.ds(256, 128)].astype(F32)
        t = jnp.sum(jnp.where(sel, t, 0.0), axis=1, keepdims=True)
        scale_buf[pl.ds(pl.multiple_of(16 * b, 16), 16), :] = jnp.broadcast_to(
            lax.rsqrt(t / D_ALL + 1e-06), (16, 128)
        )
        return carry

    lax.fori_loop(0, 16, norm, 0)
    own_scale = scale_buf[pl.ds(pl.multiple_of(16 * (2 * y + xl), 16), 16), pl.ds(0, 1)]
    fh_out[...] = (m_buf[:, pl.ds(0, WID)] * own_scale * g_in[...]).astype(BF16)

    acc[...] = jnp.zeros_like(acc)

    def logits(s, carry):
        parts = []
        for b in range(16):
            w2, p2 = slot(b // 2, 2 * (s // 8) + b % 2, lax.rem(s, 8))
            parts.append(h_buf[w2, p2])
        lhs = jnp.concatenate(parts, axis=0)
        for c in range(2):
            acc[c] += jnp.dot(lhs, e_buf[c, s], preferred_element_type=F32)
        return carry

    lax.fori_loop(0, 16, logits, 0)
    scale = scale_buf[:, pl.ds(0, 1)]
    lt = jnp.concatenate([(acc[c] * scale).T for c in range(2)], axis=0)
    top = jnp.max(lt, axis=0, keepdims=True)
    lse = top + jnp.log(jnp.sum(jnp.exp(lt - top), axis=0, keepdims=True))
    ids = lax.broadcasted_iota(jnp.int32, (2 * COLS, 256), 0) + (sec * 32 + tp - core) * COLS
    tgt = jnp.sum(jnp.where(ids == t_in[...], lt, 0.0), axis=0, keepdims=True)

    def put(ref, lse, tgt):
        ref[0:1, :] = lse[:, 0:128]
        ref[1:2, :] = lse[:, 128:256]
        ref[2:3, :] = tgt[:, 0:128]
        ref[3:4, :] = tgt[:, 128:256]

    def merge(ref, n):
        ls = ref[:, 0:2, :]
        top = jnp.max(ls, axis=0)
        return top + jnp.log(jnp.sum(jnp.exp(ls - top[None]), axis=0)), jnp.sum(ref[:, 2:4, :], axis=0)

    put(st1.at[w], lse, tgt)

    def s1_copy(i):
        return send(st1.at[w], st1.at[w], s1_s.at[i], s1_r.at[i], line_dev(i))

    def s2_copy(i):
        return send(st2.at[x * 8 + u], st2.at[x * 8 + u], s2_s.at[i], s2_r.at[i], plane_dev(i))

    def starter(copy):
        def go(i, carry):
            copy(i).start()
            return carry
        return go

    def waiter(copy):
        def go(i, carry):
            copy(i).wait_recv()
            return carry
        return go

    def ender(copy):
        def go(i, carry):
            copy(i).wait_send()
            return carry
        return go

    lax.fori_loop(1, 8, starter(s1_copy), 0)
    lax.fori_loop(1, 8, waiter(s1_copy), 0)
    ls1, tg1 = merge(st1, 8)
    st2[x * 8 + u, 0:2, :] = ls1
    st2[x * 8 + u, 2:4, :] = tg1
    lax.fori_loop(1, 32, starter(s2_copy), 0)
    lax.fori_loop(1, 32, waiter(s2_copy), 0)
    ls2, tg2 = merge(st2, 32)
    res[core] = tg2 - ls2
    c_res = send(res.at[core], res.at[core], core_s.at[2], core_r.at[2], sibling)
    c_res.start()

    c_pair.wait_send()
    c_emb.wait_send()
    lax.fori_loop(1, 16, ender(rs_copy), 0)
    lax.fori_loop(1, 32, ender(pl_copy), 0)
    for cp in sent:
        cp.wait_send()
    lax.fori_loop(1, 8, ender(s1_copy), 0)
    lax.fori_loop(1, 32, ender(s2_copy), 0)
    c_res.wait()
    lp_out[...] = res[...]


def body(resid, act, w_down, gain, embed, targets):
    anyspec = pl.BlockSpec(memory_space=pl.ANY)
    vmem = pl.BlockSpec(memory_space=pltpu.VMEM)
    dma = pltpu.SemaphoreType.DMA
    fh, lp = pl.pallas_call(
        kernel,
        out_shape=(
            jax.ShapeDtypeStruct((16, WID), BF16),
            jax.ShapeDtypeStruct((2, 2, 128), F32),
        ),
        in_specs=[anyspec] * 6,
        out_specs=(vmem, vmem),
        scratch_shapes=[
            pltpu.VMEM((2, 16, 16, HID), BF16),
            pltpu.VMEM((WID, HID), BF16),
            pltpu.VMEM((16, WID), BF16),
            pltpu.VMEM((1, WID), F32),
            pltpu.VMEM((1, 256), jnp.int32),
            pltpu.VMEM((2, 16, PADW, COLS), BF16),
            pltpu.VMEM((256, PADW), F32),
            pltpu.VMEM((256, PADW), F32),
            pltpu.VMEM((256, PADW), F32),
            pltpu.VMEM((16, 5, 8, 128), F32),
            pltpu.VMEM((16, 5, 8, 128), F32),
            pltpu.VMEM((16, PADW), F32),
            pltpu.VMEM((8, 32, 16, PADW), BF16),
            pltpu.VMEM((256, 128), F32),
            pltpu.VMEM((2, 256, COLS), F32),
            pltpu.VMEM((8, 4, 128), F32),
            pltpu.VMEM((32, 4, 128), F32),
            pltpu.VMEM((2, 2, 128), F32),
            dma((7,)), dma((3,)), dma((3,)), dma((16,)), dma((16,)), dma((32,)), dma((32,)),
            dma((16,)), dma((16,)), dma((8,)), dma((8,)), dma((32,)), dma((32,)),
        ],
        compiler_params=pltpu.CompilerParams(
            collective_id=0, has_side_effects=True, vmem_limit_bytes=40 << 20
        ),
        name="ffn_vocab",
    )(
        act.reshape(16, 2, 16, HID),
        w_down.T,
        resid,
        gain.reshape(1, WID),
        embed.reshape(16, WID, COLS),
        targets.reshape(16, 2, 16).transpose(1, 0, 2).reshape(2, 1, 256),
    )
    logprob = lp.reshape(2, 16, 16).transpose(1, 0, 2).reshape(512)
    return fh, logprob


def solution(mesh):
    return jax.shard_map(
        body,
        mesh=mesh,
        in_specs=(
            P("tp", "section"),
            P(None, "tp"),
            P("tp", "section"),
            P("section"),
            P(None, ("section", "tp")),
            P(),
        ),
        out_specs=(P("tp", "section"), P()),
        check_vma=False,
    )
```

```python
import jax
import jax.numpy as jnp
from jax import lax
from jax.experimental import pallas as pl
from jax.experimental.pallas import tpu as pltpu
from jax.sharding import PartitionSpec as P

MESH = pl.DeviceIdType.MESH
F32 = jnp.float32
BF16 = jnp.bfloat16
HID, WID = 1152, 288
D_ALL = 4608
PADW = 384
COLS = 256


def send(src, dst, s_sem, r_sem, dev):
    return pltpu.make_async_remote_copy(
        src_ref=src, dst_ref=dst, send_sem=s_sem, recv_sem=r_sem, device_id=dev, device_id_type=MESH
    )


def kernel(
    act, w_down, resid, gain, embed, targets,
    fh_out, lp_out,
    a_buf, w_buf, r_in, g_in, t_in, e0, e1, e2,
    p_out, p_in, p_own, s_buf, s_in, m_buf, hx, hw, ht, lt_buf, scale_buf, acc,
    st1, st2, res,
    ld_sem, core_s, core_r, rs_s, rs_r, xp_s, xp_r, wp_s, wp_r, xl_s, xl_r, wl_s, wl_r, s1_s, s1_r, s2_s, s2_r,
):
    sec = lax.axis_index("section")
    tp = lax.axis_index("tp")
    core = lax.rem(tp, 2)
    xl = lax.rem(tp // 2, 2)
    y = tp // 4
    xh = sec // 8
    z = lax.rem(sec, 8)
    x = 2 * xh + xl
    first = core == 0
    u = jnp.where(first, y, z)
    w = jnp.where(first, z, y)

    def dev(x2, y2, z2, c2):
        return ((x2 // 2) * 8 + z2, (y2 * 2 + lax.rem(x2, 2)) * 2 + c2)

    sibling = dev(x, y, z, 1 - core)

    def rs_peer(i):
        return lax.rem(y + i // 2, 8), lax.rem(xl + i, 2)

    def rs_dev(i):
        y2, xl2 = rs_peer(i)
        return dev(2 * xh + xl2, y2, z, core)

    def grid_dev(x2, u2, w2):
        return dev(x2, jnp.where(first, u2, w2), jnp.where(first, w2, u2), core)

    def plane_dev(i):
        return grid_dev(lax.rem(x + i // 8, 4), lax.rem(u + i, 8), w)

    def yz_dev(i):
        return dev(x, lax.rem(y + i // 8, 8), lax.rem(z + i, 8), core)

    def x_dev(k):
        return dev(2 * lax.rem(xh + k // 2, 2) + lax.rem(xl + k, 2), y, z, core)

    def line_dev(i):
        return grid_dev(x, u, lax.rem(w + i, 8))

    def load(src, dst, k):
        return pltpu.make_async_copy(src, dst, ld_sem.at[k])

    l_w = load(w_down, w_buf, 0)
    l_a0 = load(act.at[:, 1 - core], a_buf.at[0], 1)
    l_a1 = load(act.at[:, core], a_buf.at[1], 2)
    l_r = load(resid, r_in, 3)
    l_g = load(gain, g_in, 4)
    l_t = load(targets, t_in, 5)
    l_e = load(embed.at[:, pl.ds(0, 128)], e0.at[core], 6)
    l_f = load(embed.at[:, pl.ds(128, 128)], e1.at[core], 7)
    l_h = load(embed.at[:, pl.ds(256, 32)], e2.at[core], 8)
    for l in (l_w, l_a0, l_a1, l_r, l_g, l_t, l_e, l_f, l_h):
        l.start()

    barrier = pltpu.get_barrier_semaphore()
    pl.semaphore_signal(barrier, inc=1, device_id=sibling, device_id_type=MESH)

    def sig(peer):
        def go(i, carry):
            pl.semaphore_signal(barrier, inc=1, device_id=peer(i), device_id_type=MESH)
            return carry
        return go

    lax.fori_loop(0, 8, sig(lambda i: rs_dev(2 * i + 1)), 0)
    lax.fori_loop(1, 64, sig(yz_dev), 0)
    lax.fori_loop(8, 32, sig(plane_dev), 0)

    p_out[:, pl.ds(256, 128)] = jnp.zeros((256, 128), F32)
    p_own[:, pl.ds(256, 128)] = jnp.zeros((256, 128), F32)

    def partial(k):
        return lax.dot_general(
            a_buf[k].reshape(256, HID), w_buf[...], (((1,), (1,)), ((), ())), preferred_element_type=F32
        )

    l_w.wait()
    l_a0.wait()
    p_out[:, pl.ds(0, WID)] = partial(0)
    pl.semaphore_wait(barrier, 1 + 8 + 63 + 24)
    c_pair = send(p_out, p_in, core_s.at[0], core_r.at[0], sibling)
    c_pair.start()
    l_a1.wait()
    p_own[:, pl.ds(0, WID)] = partial(1)
    c_pair.wait_recv()
    for b in range(16):
        rows = pl.ds(16 * b, 16)
        v = p_own[rows, :] + p_in[rows, :]
        s_buf[b, 0] = v[0:8, 0:128]
        s_buf[b, 1] = v[0:8, 128:256]
        s_buf[b, 2] = v[8:16, 0:128]
        s_buf[b, 3] = v[8:16, 128:256]
        s_buf[b, 4] = v[0:8, 256:384] + pltpu.roll(v[8:16, 256:384], 32, 1)

    def rs_copy(i):
        y2, xl2 = rs_peer(i)
        return send(s_buf.at[y2 * 2 + xl2], s_in.at[i], rs_s.at[i], rs_r.at[i], rs_dev(i))

    def rs_start(i, carry):
        rs_copy(i).start()
        return carry

    lax.fori_loop(1, 16, rs_start, 0)

    l_e.wait()
    l_f.wait()
    l_h.wait()
    c_emb = [
        send(e.at[core], e.at[core], core_s.at[k], core_r.at[k], sibling)
        for k, e in ((1, e0), (2, e1), (3, e2))
    ]
    for cp in c_emb:
        cp.start()
    l_r.wait()
    l_g.wait()
    l_t.wait()

    def rs_wait(i, carry):
        rs_copy(i).wait_recv()
        return carry

    lax.fori_loop(1, 16, rs_wait, 0)
    total = s_buf[y * 2 + xl]
    for i in range(1, 16):
        total = total + s_in[i]
    lane8 = lax.broadcasted_iota(jnp.int32, (8, 128), 1)
    m_buf[0:8, 0:128] = total[0]
    m_buf[0:8, 128:256] = total[1]
    m_buf[8:16, 0:128] = total[2]
    m_buf[8:16, 128:256] = total[3]
    m_buf[0:8, 256:384] = jnp.where(lane8 < 32, total[4], 0.0)
    m_buf[8:16, 256:384] = jnp.where(lane8 < 32, pltpu.roll(total[4], 96, 1), 0.0)
    g_row = g_in[...].reshape(1, WID)
    mixed = m_buf[:, pl.ds(0, WID)] + r_in[...].astype(F32)
    m_buf[:, pl.ds(0, WID)] = mixed
    sq = jnp.sum(mixed * mixed, axis=1, keepdims=True)
    sq_hi = sq.astype(BF16).astype(F32)
    sq_rest = sq - sq_hi
    sq_mid = sq_rest.astype(BF16).astype(F32)
    sq_lo = (sq_rest - sq_mid).astype(BF16).astype(F32)
    lane = lax.broadcasted_iota(jnp.int32, (16, 128), 1)
    tail = jnp.where(lane == 32, sq_hi, jnp.where(lane == 33, sq_mid, jnp.where(lane == 34, sq_lo, 0.0)))
    piece = (mixed * g_row).astype(BF16)
    w_own = hw.at[w, x * 8 + u]
    w_own[:, pl.ds(128, 128)] = tail.astype(BF16)
    w_own[:, pl.ds(0, 160)] = piece[:, 128:288]
    hx[x, z * 8 + y] = piece[:, 0:128]

    def starter(copy):
        def go(i, carry):
            copy(i).start()
            return carry
        return go

    def waiter(copy):
        def go(i, carry):
            copy(i).wait_recv()
            return carry
        return go

    def ender(copy):
        def go(i, carry):
            copy(i).wait_send()
            return carry
        return go

    def wp_copy(i):
        at = hw.at[w, x * 8 + u]
        return send(at, at, wp_s.at[i], wp_r.at[i], plane_dev(i))

    def xp_copy(i):
        at = hx.at[x, z * 8 + y]
        return send(at, at, xp_s.at[i], xp_r.at[i], yz_dev(i))

    def x_copy(k, z2):
        block = hx.at[x, pl.ds(pl.multiple_of(z2 * 8, 8), 8)]
        return send(block, block, xl_s.at[k * 8 + z2], xl_r.at[k * 8 + z2], x_dev(k))

    def x_forward(dz):
        def go(i, carry):
            xp_copy(8 * i + dz).wait_recv()
            return carry
        lax.fori_loop(0 if dz else 1, 8, go, 0)
        z2 = lax.rem(z + 8 - dz, 8)
        for k in (1, 2, 3):
            x_copy(k, z2).start()

    lax.fori_loop(1, 32, starter(wp_copy), 0)
    for dz in (0, 1, 7, 2, 6, 3, 5, 4):
        def go(i, carry, dz=dz):
            xp_copy(8 * i + dz).start()
            return carry
        lax.fori_loop(0 if dz else 1, 8, go, 0)
    for dz in (0, 1, 7):
        x_forward(dz)
    lax.fori_loop(1, 32, waiter(wp_copy), 0)

    for c in range(2):
        squares = jnp.zeros((16, 128), F32)
        for j in range(4):
            tails = jnp.zeros((16, 128), F32)
            for i in range(4):
                q = 4 * j + i
                t = hw[w, 16 * c + q, :, pl.ds(128, 128)].astype(F32)
                tails = jnp.where(lane // 32 == i, pltpu.roll(t, 32 * i, 1) if i else t, tails)
                squares = jnp.where(
                    lane // 4 == q, pltpu.roll(t, (4 * q - 32) % 128, 1) if q != 8 else t, squares
                )
            ht[w, c, j] = tails.astype(BF16)
        ht[w, c, 4] = squares.astype(BF16)

    def w_copies(kind, c):
        step = (1, 7, 2, 6, 1, 7, 2, 6)[kind]
        at = lax.rem(w + (0, 0, 0, 0, 6, 2, 6, 2)[kind], 8)
        to = line_dev(step)
        slot_ = min(kind, 6) * 4 + c * 2
        main = hw.at[at, pl.ds(16 * c, 16), :, pl.ds(0, 128)]
        rest = ht.at[at, c]
        return [
            send(main, main, wl_s.at[slot_], wl_r.at[slot_], to),
            send(rest, rest, wl_s.at[slot_ + 1], wl_r.at[slot_ + 1], to),
        ]

    sent = []

    def w_send(kind, c):
        for cp in w_copies(kind, c):
            cp.start()
            sent.append(cp)

    def w_wait(kind, c):
        for cp in w_copies(kind, c):
            cp.wait_recv()

    for c in range(2):
        for kind in (2, 3):
            w_send(kind, c)
    for c in range(2):
        for kind in (0, 1):
            w_send(kind, c)

    for dz in (2, 6, 3, 5, 4):
        x_forward(dz)
    for c in range(2):
        for kind in (2, 3):
            w_wait(kind, c)
            w_send(kind + 2, c)
            if kind - 2 == c:
                w_send(kind + 4, c)

    acc[...] = jnp.zeros_like(acc)
    for cp in c_emb:
        cp.wait_recv()

    def slot(y2, x2, z2):
        return jnp.where(first, z2, y2), x2 * 8 + jnp.where(first, y2, z2)

    def add_product(lhs, e, s, n):
        for c in range(2):
            rhs = e[c, pl.ds(s, n)].reshape(256, COLS)
            acc[c] += jnp.dot(lhs, rhs, preferred_element_type=F32)

    def x_part(h2):
        def go(p, carry):
            cols = []
            for k in range(2):
                cols.append(
                    jnp.concatenate([hx[2 * h2 + b % 2, (2 * p + k) * 8 + b // 2] for b in range(16)], axis=0)
                )
            add_product(jnp.concatenate(cols, axis=1), e0, h2 * 8 + 2 * p, 2)
            return carry
        return go

    def w_part(h2):
        def go(p, carry):
            cols = []
            for k in range(2):
                tiles = []
                for b in range(16):
                    w2, p2 = slot(b // 2, 2 * h2 + b % 2, 2 * p + k)
                    tiles.append(hw[w2, p2, :, pl.ds(0, 128)])
                cols.append(jnp.concatenate(tiles, axis=0))
            add_product(jnp.concatenate(cols, axis=1), e1, h2 * 8 + 2 * p, 2)
            return carry
        return go

    def x_wait(k):
        def go(z2, carry):
            x_copy(k, z2).wait_recv()
            return carry
        lax.fori_loop(0, 8, go, 0)

    x_wait(1)
    lax.fori_loop(0, 4, x_part(xh), 0)
    x_wait(2)
    x_wait(3)
    lax.fori_loop(0, 4, x_part(1 - xh), 0)
    for c in range(2):
        for kind in (0, 1, 4, 5, 6):
            w_wait(kind, c)
        lax.fori_loop(0, 4, w_part(c), 0)

    @pl.when(first)
    def _():
        for h2 in range(2):
            for xl2 in range(2):
                for yq in range(2):
                    for zg in range(2):
                        src = [ht[4 * zg + i, h2, xl2 * 2 + yq].astype(F32) for i in range(4)]
                        for yi in range(4):
                            t = src[0]
                            for i in range(4):
                                by = 32 * ((i - yi) % 4)
                                moved = pltpu.roll(src[i], by, 1) if by else src[i]
                                t = jnp.where(lane // 32 == i, moved, t)
                            b = 2 * (4 * yq + yi) + xl2
                            lt_buf[pl.ds(16 * b, 16), pl.ds(128 * (2 * h2 + zg), 128)] = t.astype(BF16)

    @pl.when(jnp.logical_not(first))
    def _():
        for h2 in range(2):
            for b in range(16):
                for zg in range(2):
                    lt_buf[pl.ds(16 * b, 16), pl.ds(128 * (2 * h2 + zg), 128)] = ht[b // 2, h2, (b % 2) * 2 + zg]

    for h2 in range(2):
        add_product(lt_buf[:, pl.ds(256 * h2, 256)], e2, 8 * h2, 8)

    both = [ht[w2, 0, 4].astype(F32) + ht[w2, 1, 4].astype(F32) for w2 in range(8)]
    everything = both[0]
    for w2 in range(1, 8):
        everything = everything + both[w2]
    key = jnp.where(first, lane // 4, lane // 32)
    for b in range(16):
        t = jnp.where(first, everything, both[b // 2])
        mine = key == jnp.where(first, (b % 2) * 8 + b // 2, b % 2)
        t = jnp.sum(jnp.where(mine, t, 0.0), axis=1, keepdims=True)
        scale_buf[pl.ds(16 * b, 16), :] = jnp.broadcast_to(lax.rsqrt(t / D_ALL + 1e-06), (16, 128))
    own_scale = scale_buf[pl.ds(pl.multiple_of(16 * (2 * y + xl), 16), 16), pl.ds(0, 1)]
    fh_out[...] = (m_buf[:, pl.ds(0, WID)] * own_scale * g_row).astype(BF16)

    scale = scale_buf[:, pl.ds(0, 1)]
    lt = jnp.concatenate([(acc[c] * scale).T for c in range(2)], axis=0)
    top = jnp.max(lt, axis=0, keepdims=True)
    lse = top + jnp.log(jnp.sum(jnp.exp(lt - top), axis=0, keepdims=True))
    lane4 = lax.broadcasted_iota(jnp.int32, (4, 128), 1)
    lane1 = lax.broadcasted_iota(jnp.int32, (1, 128), 1)
    ids4 = t_in[...]
    ids4 = jnp.where(first, ids4, pltpu.roll(ids4, 112, 1))
    half = jnp.zeros((4, 128), jnp.int32)
    for m in range(4):
        moved = ids4 if m == 0 else pltpu.roll(ids4, 128 - 16 * m, 1)
        half = jnp.where(lane4 // 16 == m, moved, half)
    far = pltpu.roll(half, 64, 1)
    own_ids = jnp.concatenate(
        [jnp.where(lane1 < 64, half[2 * r : 2 * r + 1], far[2 * r + 1 : 2 * r + 2]) for r in range(2)], axis=1
    )
    ids = lax.broadcasted_iota(jnp.int32, (2 * COLS, 256), 0) + (sec * 32 + tp - core) * COLS
    tgt = jnp.sum(jnp.where(ids == own_ids, lt, 0.0), axis=0, keepdims=True)

    def put(ref, lse, tgt):
        ref[0:1, :] = lse[:, 0:128]
        ref[1:2, :] = lse[:, 128:256]
        ref[2:3, :] = tgt[:, 0:128]
        ref[3:4, :] = tgt[:, 128:256]

    def merge(ref, n):
        ls = ref[:, 0:2, :]
        top = jnp.max(ls, axis=0)
        return top + jnp.log(jnp.sum(jnp.exp(ls - top[None]), axis=0)), jnp.sum(ref[:, 2:4, :], axis=0)

    put(st1.at[w], lse, tgt)

    def s1_copy(i):
        return send(st1.at[w], st1.at[w], s1_s.at[i], s1_r.at[i], line_dev(i))

    def s2_copy(i):
        return send(st2.at[x * 8 + u], st2.at[x * 8 + u], s2_s.at[i], s2_r.at[i], plane_dev(i))

    lax.fori_loop(1, 8, starter(s1_copy), 0)
    lax.fori_loop(1, 8, waiter(s1_copy), 0)
    ls1, tg1 = merge(st1, 8)
    st2[x * 8 + u, 0:2, :] = ls1
    st2[x * 8 + u, 2:4, :] = tg1
    lax.fori_loop(1, 32, starter(s2_copy), 0)
    lax.fori_loop(1, 32, waiter(s2_copy), 0)
    ls2, tg2 = merge(st2, 32)
    lp = tg2 - ls2
    turned = pltpu.roll(lp, 64, 1)
    rows4 = jnp.concatenate([lp[0:1], turned[0:1], lp[1:2], turned[1:2]], axis=0)
    wide = jnp.zeros((4, 128), F32)
    for m in range(4):
        moved = rows4 if m == 0 else pltpu.roll(rows4, 16 * m, 1)
        wide = jnp.where(lane4 // 16 == 2 * m, moved, wide)
    res[core] = jnp.where(first, wide, pltpu.roll(wide, 16, 1))
    c_res = send(res.at[core], res.at[core], core_s.at[4], core_r.at[4], sibling)
    c_res.start()

    c_pair.wait_send()
    for cp in c_emb:
        cp.wait_send()
    lax.fori_loop(1, 16, ender(rs_copy), 0)
    lax.fori_loop(1, 32, ender(wp_copy), 0)
    lax.fori_loop(1, 64, ender(xp_copy), 0)
    for k in (1, 2, 3):
        def x_end(z2, carry, k=k):
            x_copy(k, z2).wait_send()
            return carry
        lax.fori_loop(0, 8, x_end, 0)
    for cp in sent:
        cp.wait_send()
    lax.fori_loop(1, 8, ender(s1_copy), 0)
    lax.fori_loop(1, 32, ender(s2_copy), 0)
    c_res.wait()
    lp_out[...] = res[0] + res[1]


def hand_on(fh, lp, fh_out, lp_out, sem):
    a = pltpu.make_async_copy(fh, fh_out, sem.at[0])
    b = pltpu.make_async_copy(lp, lp_out, sem.at[1])
    a.start()
    b.start()
    a.wait()
    b.wait()


def body(resid, act, w_down, gain, embed, targets):
    anyspec = pl.BlockSpec(memory_space=pl.ANY)
    vmem = pl.BlockSpec(memory_space=pltpu.VMEM)
    dma = pltpu.SemaphoreType.DMA
    fh, lp = pl.pallas_call(
        kernel,
        out_shape=(
            jax.ShapeDtypeStruct((16, WID), BF16),
            jax.ShapeDtypeStruct((4, 128), F32),
        ),
        in_specs=[anyspec] * 6,
        out_specs=(vmem, vmem),
        scratch_shapes=[
            pltpu.VMEM((2, 16, 16, HID), BF16),
            pltpu.VMEM((WID, HID), BF16),
            pltpu.VMEM((16, WID), BF16),
            pltpu.VMEM((WID,), F32),
            pltpu.VMEM((4, 128), jnp.int32),
            pltpu.VMEM((2, 16, 128, COLS), BF16),
            pltpu.VMEM((2, 16, 128, COLS), BF16),
            pltpu.VMEM((2, 16, 32, COLS), BF16),
            pltpu.VMEM((256, PADW), F32),
            pltpu.VMEM((256, PADW), F32),
            pltpu.VMEM((256, PADW), F32),
            pltpu.VMEM((16, 5, 8, 128), F32),
            pltpu.VMEM((16, 5, 8, 128), F32),
            pltpu.VMEM((16, PADW), F32),
            pltpu.VMEM((4, 64, 16, 128), BF16),
            pltpu.VMEM((8, 32, 16, 256), BF16),
            pltpu.VMEM((8, 2, 5, 16, 128), BF16),
            pltpu.VMEM((256, 512), BF16),
            pltpu.VMEM((256, 128), F32),
            pltpu.VMEM((2, 256, COLS), F32),
            pltpu.VMEM((8, 4, 128), F32),
            pltpu.VMEM((32, 4, 128), F32),
            pltpu.VMEM((2, 4, 128), F32),
            dma((9,)), dma((5,)), dma((5,)), dma((16,)), dma((16,)), dma((64,)), dma((64,)), dma((32,)), dma((32,)),
            dma((32,)), dma((32,)), dma((28,)), dma((28,)), dma((8,)), dma((8,)), dma((32,)), dma((32,)),
        ],
        compiler_params=pltpu.CompilerParams(
            collective_id=0, has_side_effects=True, vmem_limit_bytes=60 << 20
        ),
        name="ffn_vocab",
    )(
        act.reshape(16, 2, 16, HID),
        w_down.T,
        resid,
        gain,
        embed.reshape(16, WID, COLS),
        targets.reshape(4, 128),
    )
    fh, lp = pl.pallas_call(
        hand_on,
        out_shape=(
            jax.ShapeDtypeStruct((16, WID), BF16),
            jax.ShapeDtypeStruct((4, 128), F32),
        ),
        in_specs=[anyspec] * 2,
        out_specs=(anyspec, anyspec),
        scratch_shapes=[dma((2,))],
        name="hand_on",
    )(fh, lp)
    return fh, lp.reshape(512)


def solution(mesh):
    return jax.shard_map(
        body,
        mesh=mesh,
        in_specs=(
            P("tp", "section"),
            P(None, "tp"),
            P("tp", "section"),
            P("section"),
            P(None, ("section", "tp")),
            P(),
        ),
        out_specs=(P("tp", "section"), P()),
        check_vma=False,
    )
```

```python
import jax
import jax.numpy as jnp
from jax import lax
from jax.experimental import pallas as pl
from jax.experimental.pallas import tpu as pltpu
from jax.sharding import PartitionSpec as P

MESH = pl.DeviceIdType.MESH
F32 = jnp.float32
BF16 = jnp.bfloat16
HID, WID = 1152, 288
D_ALL = 4608
PADW = 384
COLS = 256


def send(src, dst, s_sem, r_sem, dev):
    return pltpu.make_async_remote_copy(
        src_ref=src, dst_ref=dst, send_sem=s_sem, recv_sem=r_sem, device_id=dev, device_id_type=MESH
    )


def kernel(
    act, w_down, resid, gain, embed, targets,
    fh_out, lp_out,
    a_buf, w_buf, r_in, g_in, t_in, e0, e1, e2,
    p_out, p_in, p_own, s_buf, s_in, m_buf, hx, hw, ht, lt_buf, scale_buf, acc,
    st1, st2, res,
    ld_sem, core_s, core_r, rs_s, rs_r, xp_s, xp_r, wp_s, wp_r, xl_s, xl_r, wl_s, wl_r, s1_s, s1_r, s2_s, s2_r,
):
    sec = lax.axis_index("section")
    tp = lax.axis_index("tp")
    core = lax.rem(tp, 2)
    xl = lax.rem(tp // 2, 2)
    y = tp // 4
    xh = sec // 8
    z = lax.rem(sec, 8)
    x = 2 * xh + xl
    first = core == 0
    u = jnp.where(first, y, z)
    w = jnp.where(first, z, y)

    def dev(x2, y2, z2, c2):
        return ((x2 // 2) * 8 + z2, (y2 * 2 + lax.rem(x2, 2)) * 2 + c2)

    sibling = dev(x, y, z, 1 - core)

    def rs_peer(i):
        return lax.rem(y + i // 2, 8), lax.rem(xl + i, 2)

    def rs_dev(i):
        y2, xl2 = rs_peer(i)
        return dev(2 * xh + xl2, y2, z, core)

    def grid_dev(x2, u2, w2):
        return dev(x2, jnp.where(first, u2, w2), jnp.where(first, w2, u2), core)

    def plane_dev(i):
        return grid_dev(lax.rem(x + i // 8, 4), lax.rem(u + i, 8), w)

    def u_dev(i):
        return grid_dev(x, lax.rem(u + i, 8), w)

    def x_dev(k):
        return dev(2 * lax.rem(xh + k // 2, 2) + lax.rem(xl + k, 2), y, z, core)

    def line_dev(i):
        return grid_dev(x, u, lax.rem(w + i, 8))

    def load(src, dst, k):
        return pltpu.make_async_copy(src, dst, ld_sem.at[k])

    l_w = load(w_down, w_buf, 0)
    l_a0 = load(act.at[:, 1 - core], a_buf.at[0], 1)
    l_a1 = load(act.at[:, core], a_buf.at[1], 2)
    l_r = load(resid, r_in, 3)
    l_g = load(gain, g_in, 4)
    l_t = load(targets, t_in, 5)
    l_e = load(embed.at[:, pl.ds(0, 128)], e0.at[core], 6)
    l_f = load(embed.at[:, pl.ds(128, 128)], e1.at[core], 7)
    l_h = load(embed.at[:, pl.ds(256, 32)], e2.at[core], 8)
    for l in (l_w, l_a0, l_a1, l_r, l_g, l_t, l_e, l_f, l_h):
        l.start()

    barrier = pltpu.get_barrier_semaphore()
    pl.semaphore_signal(barrier, inc=1, device_id=sibling, device_id_type=MESH)

    def sig(peer):
        def go(i, carry):
            pl.semaphore_signal(barrier, inc=1, device_id=peer(i), device_id_type=MESH)
            return carry
        return go

    lax.fori_loop(0, 8, sig(lambda i: rs_dev(2 * i + 1)), 0)
    lax.fori_loop(1, 8, sig(line_dev), 0)
    lax.fori_loop(1, 32, sig(plane_dev), 0)

    p_out[:, pl.ds(256, 128)] = jnp.zeros((256, 128), F32)
    p_own[:, pl.ds(256, 128)] = jnp.zeros((256, 128), F32)

    def partial(k):
        return lax.dot_general(
            a_buf[k].reshape(256, HID), w_buf[...], (((1,), (1,)), ((), ())), preferred_element_type=F32
        )

    l_w.wait()
    l_a0.wait()
    p_out[:, pl.ds(0, WID)] = partial(0)
    pl.semaphore_wait(barrier, 1 + 8 + 7 + 31)
    c_pair = send(p_out, p_in, core_s.at[0], core_r.at[0], sibling)
    c_pair.start()
    l_a1.wait()
    p_own[:, pl.ds(0, WID)] = partial(1)
    c_pair.wait_recv()
    for b in range(16):
        rows = pl.ds(16 * b, 16)
        v = p_own[rows, :] + p_in[rows, :]
        s_buf[b, 0] = v[0:8, 0:128]
        s_buf[b, 1] = v[0:8, 128:256]
        s_buf[b, 2] = v[8:16, 0:128]
        s_buf[b, 3] = v[8:16, 128:256]
        s_buf[b, 4] = v[0:8, 256:384] + pltpu.roll(v[8:16, 256:384], 32, 1)

    def rs_copy(i):
        y2, xl2 = rs_peer(i)
        return send(s_buf.at[y2 * 2 + xl2], s_in.at[i], rs_s.at[i], rs_r.at[i], rs_dev(i))

    def rs_start(i, carry):
        rs_copy(i).start()
        return carry

    for i in (8, 9, 6, 7, 10, 11, 4, 5, 12, 13, 2, 3, 14, 15, 1):
        rs_copy(i).start()

    l_e.wait()
    l_f.wait()
    l_h.wait()
    c_emb = [
        send(e.at[core], e.at[core], core_s.at[k], core_r.at[k], sibling)
        for k, e in ((1, e0), (2, e1), (3, e2))
    ]
    for cp in c_emb:
        cp.start()
    l_r.wait()
    l_g.wait()
    l_t.wait()

    def rs_wait(i, carry):
        rs_copy(i).wait_recv()
        return carry

    lax.fori_loop(1, 16, rs_wait, 0)
    total = s_buf[y * 2 + xl]
    for i in range(1, 16):
        total = total + s_in[i]
    lane8 = lax.broadcasted_iota(jnp.int32, (8, 128), 1)
    m_buf[0:8, 0:128] = total[0]
    m_buf[0:8, 128:256] = total[1]
    m_buf[8:16, 0:128] = total[2]
    m_buf[8:16, 128:256] = total[3]
    m_buf[0:8, 256:384] = jnp.where(lane8 < 32, total[4], 0.0)
    m_buf[8:16, 256:384] = jnp.where(lane8 < 32, pltpu.roll(total[4], 96, 1), 0.0)
    g_row = g_in[...].reshape(1, WID)
    mixed = m_buf[:, pl.ds(0, WID)] + r_in[...].astype(F32)
    m_buf[:, pl.ds(0, WID)] = mixed
    sq = jnp.sum(mixed * mixed, axis=1, keepdims=True)
    sq_hi = sq.astype(BF16).astype(F32)
    sq_rest = sq - sq_hi
    sq_mid = sq_rest.astype(BF16).astype(F32)
    sq_lo = (sq_rest - sq_mid).astype(BF16).astype(F32)
    lane = lax.broadcasted_iota(jnp.int32, (16, 128), 1)
    tail = jnp.where(lane == 32, sq_hi, jnp.where(lane == 33, sq_mid, jnp.where(lane == 34, sq_lo, 0.0)))
    piece = (mixed * g_row).astype(BF16)
    w_own = hw.at[w, x * 8 + u]
    w_own[:, pl.ds(128, 128)] = tail.astype(BF16)
    w_own[:, pl.ds(0, 160)] = piece[:, 128:288]
    hx[x, w * 8 + u] = piece[:, 0:128]

    def starter(copy):
        def go(i, carry):
            copy(i).start()
            return carry
        return go

    def waiter(copy):
        def go(i, carry):
            copy(i).wait_recv()
            return carry
        return go

    def ender(copy):
        def go(i, carry):
            copy(i).wait_send()
            return carry
        return go

    def wp_copy(i):
        at = hw.at[w, x * 8 + u]
        return send(at, at, wp_s.at[i], wp_r.at[i], plane_dev(i))

    def xu_copy(i):
        at = hx.at[x, w * 8 + u]
        return send(at, at, xp_s.at[i], xp_r.at[i], u_dev(i))

    def chunk(w2):
        return hx.at[x, pl.ds(pl.multiple_of(w2 * 8, 8), 8)]

    def xw_copy(j):
        return send(chunk(w), chunk(w), xp_s.at[8 + j], xp_r.at[8 + j], line_dev(j))

    def x_copy(k, w2):
        return send(chunk(w2), chunk(w2), xl_s.at[k * 8 + w2], xl_r.at[k * 8 + w2], x_dev(k))

    def x_forward(j):
        xw_copy(j).wait_recv()
        for k in (1, 2, 3):
            x_copy(k, lax.rem(w + 8 - j, 8)).start()

    lax.fori_loop(1, 8, starter(xu_copy), 0)
    for du in (4, 3, 5, 2, 6, 1, 7, 0):
        for dx in (2, 1, 3, 0):
            if du or dx:
                wp_copy(8 * dx + du).start()
    lax.fori_loop(1, 8, waiter(xu_copy), 0)
    for j in (4, 3, 5, 2, 6, 1, 7):
        xw_copy(j).start()
    for k in (1, 2, 3):
        x_copy(k, w).start()
    lax.fori_loop(1, 32, waiter(wp_copy), 0)

    for c in range(2):
        squares = jnp.zeros((16, 128), F32)
        for j in range(4):
            tails = jnp.zeros((16, 128), F32)
            for i in range(4):
                q = 4 * j + i
                t = hw[w, 16 * c + q, :, pl.ds(128, 128)].astype(F32)
                tails = jnp.where(lane // 32 == i, pltpu.roll(t, 32 * i, 1) if i else t, tails)
                squares = jnp.where(
                    lane // 4 == q, pltpu.roll(t, (4 * q - 32) % 128, 1) if q != 8 else t, squares
                )
            ht[w, c, j] = tails.astype(BF16)
        ht[w, c, 4] = squares.astype(BF16)

    def w_copies(kind, c):
        step = (1, 7, 2, 6, 1, 7, 2, 6)[kind]
        at = lax.rem(w + (0, 0, 0, 0, 6, 2, 6, 2)[kind], 8)
        to = line_dev(step)
        slot_ = min(kind, 6) * 4 + c * 2
        main = hw.at[at, pl.ds(16 * c, 16), :, pl.ds(0, 128)]
        rest = ht.at[at, c]
        return [
            send(main, main, wl_s.at[slot_], wl_r.at[slot_], to),
            send(rest, rest, wl_s.at[slot_ + 1], wl_r.at[slot_ + 1], to),
        ]

    sent = []

    def w_send(kind, c):
        for cp in w_copies(kind, c):
            cp.start()
            sent.append(cp)

    def w_wait(kind, c):
        for cp in w_copies(kind, c):
            cp.wait_recv()

    for c in range(2):
        for kind in (2, 3):
            w_send(kind, c)
    for c in range(2):
        for kind in (0, 1):
            w_send(kind, c)

    for j in (1, 7, 2, 6, 3, 5, 4):
        x_forward(j)
    for c in range(2):
        for kind in (2, 3):
            w_wait(kind, c)
            w_send(kind + 2, c)
            if kind - 2 == c:
                w_send(kind + 4, c)

    acc[...] = jnp.zeros_like(acc)
    for cp in c_emb:
        cp.wait_recv()

    def slot(y2, x2, z2):
        return jnp.where(first, z2, y2), x2 * 8 + jnp.where(first, y2, z2)

    def place(y2, z2):
        return jnp.where(first, z2 * 8 + y2, y2 * 8 + z2)

    def add_product(lhs, e, s, n):
        for c in range(2):
            rhs = e[c, pl.ds(s, n)].reshape(256, COLS)
            acc[c] += jnp.dot(lhs, rhs, preferred_element_type=F32)

    def x_part(h2):
        def go(p, carry):
            cols = []
            for k in range(2):
                cols.append(
                    jnp.concatenate([hx[2 * h2 + b % 2, place(b // 2, 2 * p + k)] for b in range(16)], axis=0)
                )
            add_product(jnp.concatenate(cols, axis=1), e0, h2 * 8 + 2 * p, 2)
            return carry
        return go

    def w_part(h2):
        def go(p, carry):
            cols = []
            for k in range(2):
                tiles = []
                for b in range(16):
                    w2, p2 = slot(b // 2, 2 * h2 + b % 2, 2 * p + k)
                    tiles.append(hw[w2, p2, :, pl.ds(0, 128)])
                cols.append(jnp.concatenate(tiles, axis=0))
            add_product(jnp.concatenate(cols, axis=1), e1, h2 * 8 + 2 * p, 2)
            return carry
        return go

    def x_wait(k):
        def go(z2, carry):
            x_copy(k, z2).wait_recv()
            return carry
        lax.fori_loop(0, 8, go, 0)

    x_wait(1)
    lax.fori_loop(0, 4, x_part(xh), 0)
    x_wait(2)
    x_wait(3)
    lax.fori_loop(0, 4, x_part(1 - xh), 0)
    for c in range(2):
        for kind in (0, 1, 4, 5, 6):
            w_wait(kind, c)
        lax.fori_loop(0, 4, w_part(c), 0)

    @pl.when(first)
    def _():
        for h2 in range(2):
            for xl2 in range(2):
                for yq in range(2):
                    for zg in range(2):
                        src = [ht[4 * zg + i, h2, xl2 * 2 + yq].astype(F32) for i in range(4)]
                        for yi in range(4):
                            t = src[0]
                            for i in range(4):
                                by = 32 * ((i - yi) % 4)
                                moved = pltpu.roll(src[i], by, 1) if by else src[i]
                                t = jnp.where(lane // 32 == i, moved, t)
                            b = 2 * (4 * yq + yi) + xl2
                            lt_buf[pl.ds(16 * b, 16), pl.ds(128 * (2 * h2 + zg), 128)] = t.astype(BF16)

    @pl.when(jnp.logical_not(first))
    def _():
        for h2 in range(2):
            for b in range(16):
                for zg in range(2):
                    lt_buf[pl.ds(16 * b, 16), pl.ds(128 * (2 * h2 + zg), 128)] = ht[b // 2, h2, (b % 2) * 2 + zg]

    for h2 in range(2):
        add_product(lt_buf[:, pl.ds(256 * h2, 256)], e2, 8 * h2, 8)

    both = [ht[w2, 0, 4].astype(F32) + ht[w2, 1, 4].astype(F32) for w2 in range(8)]
    everything = both[0]
    for w2 in range(1, 8):
        everything = everything + both[w2]
    key = jnp.where(first, lane // 4, lane // 32)
    for b in range(16):
        t = jnp.where(first, everything, both[b // 2])
        mine = key == jnp.where(first, (b % 2) * 8 + b // 2, b % 2)
        t = jnp.sum(jnp.where(mine, t, 0.0), axis=1, keepdims=True)
        scale_buf[pl.ds(16 * b, 16), :] = jnp.broadcast_to(lax.rsqrt(t / D_ALL + 1e-06), (16, 128))
    own_scale = scale_buf[pl.ds(pl.multiple_of(16 * (2 * y + xl), 16), 16), pl.ds(0, 1)]
    fh_out[...] = (m_buf[:, pl.ds(0, WID)] * own_scale * g_row).astype(BF16)

    scale = scale_buf[:, pl.ds(0, 1)]
    lt = jnp.concatenate([(acc[c] * scale).T for c in range(2)], axis=0)
    top = jnp.max(lt, axis=0, keepdims=True)
    lse = top + jnp.log(jnp.sum(jnp.exp(lt - top), axis=0, keepdims=True))
    lane4 = lax.broadcasted_iota(jnp.int32, (4, 128), 1)
    lane1 = lax.broadcasted_iota(jnp.int32, (1, 128), 1)
    ids4 = t_in[...]
    ids4 = jnp.where(first, ids4, pltpu.roll(ids4, 112, 1))
    half = jnp.zeros((4, 128), jnp.int32)
    for m in range(4):
        moved = ids4 if m == 0 else pltpu.roll(ids4, 128 - 16 * m, 1)
        half = jnp.where(lane4 // 16 == m, moved, half)
    far = pltpu.roll(half, 64, 1)
    own_ids = jnp.concatenate(
        [jnp.where(lane1 < 64, half[2 * r : 2 * r + 1], far[2 * r + 1 : 2 * r + 2]) for r in range(2)], axis=1
    )
    ids = lax.broadcasted_iota(jnp.int32, (2 * COLS, 256), 0) + (sec * 32 + tp - core) * COLS
    tgt = jnp.sum(jnp.where(ids == own_ids, lt, 0.0), axis=0, keepdims=True)

    def put(ref, lse, tgt):
        ref[0:1, :] = lse[:, 0:128]
        ref[1:2, :] = lse[:, 128:256]
        ref[2:3, :] = tgt[:, 0:128]
        ref[3:4, :] = tgt[:, 128:256]

    def merge(ref, n):
        ls = ref[:, 0:2, :]
        top = jnp.max(ls, axis=0)
        return top + jnp.log(jnp.sum(jnp.exp(ls - top[None]), axis=0)), jnp.sum(ref[:, 2:4, :], axis=0)

    put(st1.at[w], lse, tgt)

    def s1_copy(i):
        return send(st1.at[w], st1.at[w], s1_s.at[i], s1_r.at[i], line_dev(i))

    def s2_copy(i):
        return send(st2.at[x * 8 + u], st2.at[x * 8 + u], s2_s.at[i], s2_r.at[i], plane_dev(i))

    lax.fori_loop(1, 8, starter(s1_copy), 0)
    lax.fori_loop(1, 8, waiter(s1_copy), 0)
    ls1, tg1 = merge(st1, 8)
    st2[x * 8 + u, 0:2, :] = ls1
    st2[x * 8 + u, 2:4, :] = tg1
    lax.fori_loop(1, 32, starter(s2_copy), 0)
    lax.fori_loop(1, 32, waiter(s2_copy), 0)
    ls2, tg2 = merge(st2, 32)
    lp = tg2 - ls2
    turned = pltpu.roll(lp, 64, 1)
    rows4 = jnp.concatenate([lp[0:1], turned[0:1], lp[1:2], turned[1:2]], axis=0)
    wide = jnp.zeros((4, 128), F32)
    for m in range(4):
        moved = rows4 if m == 0 else pltpu.roll(rows4, 16 * m, 1)
        wide = jnp.where(lane4 // 16 == 2 * m, moved, wide)
    res[core] = jnp.where(first, wide, pltpu.roll(wide, 16, 1))
    c_res = send(res.at[core], res.at[core], core_s.at[4], core_r.at[4], sibling)
    c_res.start()

    c_pair.wait_send()
    for cp in c_emb:
        cp.wait_send()
    lax.fori_loop(1, 16, ender(rs_copy), 0)
    lax.fori_loop(1, 32, ender(wp_copy), 0)
    lax.fori_loop(1, 8, ender(xu_copy), 0)
    lax.fori_loop(1, 8, ender(xw_copy), 0)
    for k in (1, 2, 3):
        def x_end(z2, carry, k=k):
            x_copy(k, z2).wait_send()
            return carry
        lax.fori_loop(0, 8, x_end, 0)
    for cp in sent:
        cp.wait_send()
    lax.fori_loop(1, 8, ender(s1_copy), 0)
    lax.fori_loop(1, 32, ender(s2_copy), 0)
    c_res.wait()
    lp_out[...] = res[0] + res[1]


def hand_on(fh, lp, fh_out, lp_out, sem):
    a = pltpu.make_async_copy(fh, fh_out, sem.at[0])
    b = pltpu.make_async_copy(lp, lp_out, sem.at[1])
    a.start()
    b.start()
    a.wait()
    b.wait()


def body(resid, act, w_down, gain, embed, targets):
    anyspec = pl.BlockSpec(memory_space=pl.ANY)
    vmem = pl.BlockSpec(memory_space=pltpu.VMEM)
    dma = pltpu.SemaphoreType.DMA
    fh, lp = pl.pallas_call(
        kernel,
        out_shape=(
            jax.ShapeDtypeStruct((16, WID), BF16),
            jax.ShapeDtypeStruct((4, 128), F32),
        ),
        in_specs=[anyspec] * 6,
        out_specs=(vmem, vmem),
        scratch_shapes=[
            pltpu.VMEM((2, 16, 16, HID), BF16),
            pltpu.VMEM((WID, HID), BF16),
            pltpu.VMEM((16, WID), BF16),
            pltpu.VMEM((WID,), F32),
            pltpu.VMEM((4, 128), jnp.int32),
            pltpu.VMEM((2, 16, 128, COLS), BF16),
            pltpu.VMEM((2, 16, 128, COLS), BF16),
            pltpu.VMEM((2, 16, 32, COLS), BF16),
            pltpu.VMEM((256, PADW), F32),
            pltpu.VMEM((256, PADW), F32),
            pltpu.VMEM((256, PADW), F32),
            pltpu.VMEM((16, 5, 8, 128), F32),
            pltpu.VMEM((16, 5, 8, 128), F32),
            pltpu.VMEM((16, PADW), F32),
            pltpu.VMEM((4, 64, 16, 128), BF16),
            pltpu.VMEM((8, 32, 16, 256), BF16),
            pltpu.VMEM((8, 2, 5, 16, 128), BF16),
            pltpu.VMEM((256, 512), BF16),
            pltpu.VMEM((256, 128), F32),
            pltpu.VMEM((2, 256, COLS), F32),
            pltpu.VMEM((8, 4, 128), F32),
            pltpu.VMEM((32, 4, 128), F32),
            pltpu.VMEM((2, 4, 128), F32),
            dma((9,)), dma((5,)), dma((5,)), dma((16,)), dma((16,)), dma((16,)), dma((16,)), dma((32,)), dma((32,)),
            dma((32,)), dma((32,)), dma((28,)), dma((28,)), dma((8,)), dma((8,)), dma((32,)), dma((32,)),
        ],
        compiler_params=pltpu.CompilerParams(
            collective_id=0, has_side_effects=True, vmem_limit_bytes=60 << 20
        ),
        name="ffn_vocab",
    )(
        act.reshape(16, 2, 16, HID),
        w_down.T,
        resid,
        gain,
        embed.reshape(16, WID, COLS),
        targets.reshape(4, 128),
    )
    fh, lp = pl.pallas_call(
        hand_on,
        out_shape=(
            jax.ShapeDtypeStruct((16, WID), BF16),
            jax.ShapeDtypeStruct((4, 128), F32),
        ),
        in_specs=[anyspec] * 2,
        out_specs=(anyspec, anyspec),
        scratch_shapes=[dma((2,))],
        name="hand_on",
    )(fh, lp)
    return fh, lp.reshape(512)


def solution(mesh):
    return jax.shard_map(
        body,
        mesh=mesh,
        in_specs=(
            P("tp", "section"),
            P(None, "tp"),
            P("tp", "section"),
            P("section"),
            P(None, ("section", "tp")),
            P(),
        ),
        out_specs=(P("tp", "section"), P()),
        check_vma=False,
    )
```

```python
import jax
import jax.numpy as jnp
from jax import lax
from jax.experimental import pallas as pl
from jax.experimental.pallas import tpu as pltpu
from jax.sharding import PartitionSpec as P

MESH = pl.DeviceIdType.MESH
F32 = jnp.float32
BF16 = jnp.bfloat16
HID, WID = 1152, 288
D_ALL = 4608
PADW = 384
COLS = 256


def send(src, dst, s_sem, r_sem, dev):
    return pltpu.make_async_remote_copy(
        src_ref=src, dst_ref=dst, send_sem=s_sem, recv_sem=r_sem, device_id=dev, device_id_type=MESH
    )


def kernel(
    act, w_down, resid, gain, embed, targets,
    fh_out, lp_out,
    a_buf, w_buf, r_in, g_in, t_in, e0, e1, e2,
    p_out, p_in, p_own, s_buf, s_in, m_buf, hx, hw, ht, lt_buf, scale_buf, acc,
    st1, st2, res,
    ld_sem, core_s, core_r, rs_s, rs_r, xp_s, xp_r, wp_s, wp_r, xl_s, xl_r, wl_s, wl_r, s1_s, s1_r, s2_s, s2_r,
):
    sec = lax.axis_index("section")
    tp = lax.axis_index("tp")
    core = lax.rem(tp, 2)
    xl = lax.rem(tp // 2, 2)
    y = tp // 4
    xh = sec // 8
    z = lax.rem(sec, 8)
    x = 2 * xh + xl
    first = core == 0
    u = jnp.where(first, y, z)
    w = jnp.where(first, z, y)

    def dev(x2, y2, z2, c2):
        return ((x2 // 2) * 8 + z2, (y2 * 2 + lax.rem(x2, 2)) * 2 + c2)

    sibling = dev(x, y, z, 1 - core)

    def rs_peer(i):
        return lax.rem(y + i // 2, 8), lax.rem(xl + i, 2)

    def rs_dev(i):
        y2, xl2 = rs_peer(i)
        return dev(2 * xh + xl2, y2, z, core)

    def grid_dev(x2, u2, w2):
        return dev(x2, jnp.where(first, u2, w2), jnp.where(first, w2, u2), core)

    def plane_dev(i):
        return grid_dev(lax.rem(x + i // 8, 4), lax.rem(u + i, 8), w)

    def u_dev(i):
        return grid_dev(x, lax.rem(u + i, 8), w)

    def x_dev(k):
        return dev(2 * lax.rem(xh + k // 2, 2) + lax.rem(xl + k, 2), y, z, core)

    def line_dev(i):
        return grid_dev(x, u, lax.rem(w + i, 8))

    def load(src, dst, k):
        return pltpu.make_async_copy(src, dst, ld_sem.at[k])

    l_w = load(w_down, w_buf, 0)
    l_a0 = load(act.at[:, 1 - core], a_buf.at[0], 1)
    l_a1 = load(act.at[:, core], a_buf.at[1], 2)
    l_r = load(resid, r_in, 3)
    l_g = load(gain, g_in, 4)
    l_t = load(targets, t_in, 5)
    l_e = load(embed.at[:, pl.ds(0, 128)], e0.at[core], 6)
    l_f = load(embed.at[:, pl.ds(128, 128)], e1.at[core], 7)
    l_h = load(embed.at[:, pl.ds(256, 32)], e2.at[core], 8)
    for l in (l_w, l_a0, l_a1, l_r, l_g, l_t, l_e, l_f, l_h):
        l.start()

    barrier = pltpu.get_barrier_semaphore()
    pl.semaphore_signal(barrier, inc=1, device_id=sibling, device_id_type=MESH)

    def sig(peer):
        def go(i, carry):
            pl.semaphore_signal(barrier, inc=1, device_id=peer(i), device_id_type=MESH)
            return carry
        return go

    lax.fori_loop(0, 8, sig(lambda i: rs_dev(2 * i + 1)), 0)
    lax.fori_loop(1, 8, sig(line_dev), 0)
    lax.fori_loop(1, 32, sig(plane_dev), 0)

    p_out[:, pl.ds(256, 128)] = jnp.zeros((256, 128), F32)
    p_own[:, pl.ds(256, 128)] = jnp.zeros((256, 128), F32)

    def partial(k):
        return lax.dot_general(
            a_buf[k].reshape(256, HID), w_buf[...], (((1,), (1,)), ((), ())), preferred_element_type=F32
        )

    l_w.wait()
    l_a0.wait()
    p_out[:, pl.ds(0, WID)] = partial(0)
    pl.semaphore_wait(barrier, 1 + 8 + 7 + 31)
    c_pair = send(p_out, p_in, core_s.at[0], core_r.at[0], sibling)
    c_pair.start()
    l_a1.wait()
    p_own[:, pl.ds(0, WID)] = partial(1)
    c_pair.wait_recv()
    for b in range(16):
        rows = pl.ds(16 * b, 16)
        v = p_own[rows, :] + p_in[rows, :]
        s_buf[b, 0] = v[0:8, 0:128]
        s_buf[b, 1] = v[0:8, 128:256]
        s_buf[b, 2] = v[8:16, 0:128]
        s_buf[b, 3] = v[8:16, 128:256]
        s_buf[b, 4] = v[0:8, 256:384] + pltpu.roll(v[8:16, 256:384], 32, 1)

    def rs_copy(i):
        y2, xl2 = rs_peer(i)
        return send(s_buf.at[y2 * 2 + xl2], s_in.at[i], rs_s.at[i], rs_r.at[i], rs_dev(i))

    def rs_start(i, carry):
        rs_copy(i).start()
        return carry

    for i in (8, 9, 6, 7, 10, 11, 4, 5, 12, 13, 2, 3, 14, 15, 1):
        rs_copy(i).start()

    l_e.wait()
    l_f.wait()
    l_h.wait()
    c_emb = [
        send(e.at[core], e.at[core], core_s.at[k], core_r.at[k], sibling)
        for k, e in ((1, e0), (2, e1), (3, e2))
    ]
    for cp in c_emb:
        cp.start()
    l_r.wait()
    l_g.wait()
    l_t.wait()

    def rs_wait(i, carry):
        rs_copy(i).wait_recv()
        return carry

    lax.fori_loop(1, 16, rs_wait, 0)
    total = s_buf[y * 2 + xl]
    for i in range(1, 16):
        total = total + s_in[i]
    lane8 = lax.broadcasted_iota(jnp.int32, (8, 128), 1)
    m_buf[0:8, 0:128] = total[0]
    m_buf[0:8, 128:256] = total[1]
    m_buf[8:16, 0:128] = total[2]
    m_buf[8:16, 128:256] = total[3]
    m_buf[0:8, 256:384] = jnp.where(lane8 < 32, total[4], 0.0)
    m_buf[8:16, 256:384] = jnp.where(lane8 < 32, pltpu.roll(total[4], 96, 1), 0.0)
    g_row = g_in[...].reshape(1, WID)
    mixed = m_buf[:, pl.ds(0, WID)] + r_in[...].astype(F32)
    m_buf[:, pl.ds(0, WID)] = mixed
    sq = jnp.sum(mixed * mixed, axis=1, keepdims=True)
    sq_hi = sq.astype(BF16).astype(F32)
    sq_rest = sq - sq_hi
    sq_mid = sq_rest.astype(BF16).astype(F32)
    sq_lo = (sq_rest - sq_mid).astype(BF16).astype(F32)
    lane = lax.broadcasted_iota(jnp.int32, (16, 128), 1)
    tail = jnp.where(lane == 32, sq_hi, jnp.where(lane == 33, sq_mid, jnp.where(lane == 34, sq_lo, 0.0)))
    piece = (mixed * g_row).astype(BF16)
    w_own = hw.at[w, x * 8 + u]
    w_own[:, pl.ds(128, 128)] = tail.astype(BF16)
    w_own[:, pl.ds(0, 160)] = piece[:, 128:288]
    hx[x, w * 8 + u] = piece[:, 0:128]

    def starter(copy):
        def go(i, carry):
            copy(i).start()
            return carry
        return go

    def waiter(copy):
        def go(i, carry):
            copy(i).wait_recv()
            return carry
        return go

    def ender(copy):
        def go(i, carry):
            copy(i).wait_send()
            return carry
        return go

    def wp_copy(i):
        at = hw.at[w, x * 8 + u]
        return send(at, at, wp_s.at[i], wp_r.at[i], plane_dev(i))

    def xu_copy(i):
        at = hx.at[x, w * 8 + u]
        return send(at, at, xp_s.at[i], xp_r.at[i], u_dev(i))

    def chunk(w2):
        return hx.at[x, pl.ds(pl.multiple_of(w2 * 8, 8), 8)]

    def xw_copy(j):
        return send(chunk(w), chunk(w), xp_s.at[8 + j], xp_r.at[8 + j], line_dev(j))

    def x_copy(k, w2):
        return send(chunk(w2), chunk(w2), xl_s.at[k * 8 + w2], xl_r.at[k * 8 + w2], x_dev(k))

    def x_forward(j):
        xw_copy(j).wait_recv()
        for k in (2, 1, 3):
            x_copy(k, lax.rem(w + 8 - j, 8)).start()

    lax.fori_loop(1, 8, starter(xu_copy), 0)
    for du in (4, 3, 5, 2, 6, 1, 7, 0):
        for dx in (2, 1, 3, 0):
            if du or dx:
                wp_copy(8 * dx + du).start()
    lax.fori_loop(1, 8, waiter(xu_copy), 0)
    for j in (4, 3, 5, 2, 6, 1, 7):
        xw_copy(j).start()
    for k in (2, 1, 3):
        x_copy(k, w).start()
    lax.fori_loop(1, 32, waiter(wp_copy), 0)

    for c in range(2):
        squares = jnp.zeros((16, 128), F32)
        for j in range(4):
            tails = jnp.zeros((16, 128), F32)
            for i in range(4):
                q = 4 * j + i
                t = hw[w, 16 * c + q, :, pl.ds(128, 128)].astype(F32)
                tails = jnp.where(lane // 32 == i, pltpu.roll(t, 32 * i, 1) if i else t, tails)
                squares = jnp.where(
                    lane // 4 == q, pltpu.roll(t, (4 * q - 32) % 128, 1) if q != 8 else t, squares
                )
            ht[w, c, j] = tails.astype(BF16)
        ht[w, c, 4] = squares.astype(BF16)

    def w_copies(kind, c):
        step = (1, 7, 2, 6, 1, 7, 2, 6)[kind]
        at = lax.rem(w + (0, 0, 0, 0, 6, 2, 6, 2)[kind], 8)
        to = line_dev(step)
        slot_ = min(kind, 6) * 4 + c * 2
        main = hw.at[at, pl.ds(16 * c, 16), :, pl.ds(0, 128)]
        rest = ht.at[at, c]
        return [
            send(main, main, wl_s.at[slot_], wl_r.at[slot_], to),
            send(rest, rest, wl_s.at[slot_ + 1], wl_r.at[slot_ + 1], to),
        ]

    sent = []

    def w_send(kind, c):
        for cp in w_copies(kind, c):
            cp.start()
            sent.append(cp)

    def w_wait(kind, c):
        for cp in w_copies(kind, c):
            cp.wait_recv()

    for c in range(2):
        for kind in (2, 3, 0, 1):
            w_send(kind, c)

    for j in (1, 7, 2, 6, 3, 5, 4):
        x_forward(j)
    for c in range(2):
        for kind in (2, 3):
            w_wait(kind, c)
            w_send(kind + 2, c)
            if kind - 2 == c:
                w_send(kind + 4, c)

    acc[...] = jnp.zeros_like(acc)
    for cp in c_emb:
        cp.wait_recv()

    def slot(y2, x2, z2):
        return jnp.where(first, z2, y2), x2 * 8 + jnp.where(first, y2, z2)

    def place(y2, z2):
        return jnp.where(first, z2 * 8 + y2, y2 * 8 + z2)

    def add_product(lhs, e, s, n):
        for c in range(2):
            rhs = e[c, pl.ds(s, n)].reshape(256, COLS)
            acc[c] += jnp.dot(lhs, rhs, preferred_element_type=F32)

    def x_part(h2):
        def go(p, carry):
            cols = []
            for k in range(2):
                cols.append(
                    jnp.concatenate([hx[2 * h2 + b % 2, place(b // 2, 2 * p + k)] for b in range(16)], axis=0)
                )
            add_product(jnp.concatenate(cols, axis=1), e0, h2 * 8 + 2 * p, 2)
            return carry
        return go

    def w_part(h2):
        def go(p, carry):
            cols = []
            for k in range(2):
                tiles = []
                for b in range(16):
                    w2, p2 = slot(b // 2, 2 * h2 + b % 2, 2 * p + k)
                    tiles.append(hw[w2, p2, :, pl.ds(0, 128)])
                cols.append(jnp.concatenate(tiles, axis=0))
            add_product(jnp.concatenate(cols, axis=1), e1, h2 * 8 + 2 * p, 2)
            return carry
        return go

    def x_wait(k):
        def go(z2, carry):
            x_copy(k, z2).wait_recv()
            return carry
        lax.fori_loop(0, 8, go, 0)

    x_wait(1)
    lax.fori_loop(0, 4, x_part(xh), 0)
    x_wait(2)
    x_wait(3)
    lax.fori_loop(0, 4, x_part(1 - xh), 0)
    for c in range(2):
        for kind in (0, 1, 4, 5, 6):
            w_wait(kind, c)
        lax.fori_loop(0, 4, w_part(c), 0)

    @pl.when(first)
    def _():
        for h2 in range(2):
            for xl2 in range(2):
                for yq in range(2):
                    for zg in range(2):
                        src = [ht[4 * zg + i, h2, xl2 * 2 + yq].astype(F32) for i in range(4)]
                        for yi in range(4):
                            t = src[0]
                            for i in range(4):
                                by = 32 * ((i - yi) % 4)
                                moved = pltpu.roll(src[i], by, 1) if by else src[i]
                                t = jnp.where(lane // 32 == i, moved, t)
                            b = 2 * (4 * yq + yi) + xl2
                            lt_buf[pl.ds(16 * b, 16), pl.ds(128 * (2 * h2 + zg), 128)] = t.astype(BF16)

    @pl.when(jnp.logical_not(first))
    def _():
        for h2 in range(2):
            for b in range(16):
                for zg in range(2):
                    lt_buf[pl.ds(16 * b, 16), pl.ds(128 * (2 * h2 + zg), 128)] = ht[b // 2, h2, (b % 2) * 2 + zg]

    for h2 in range(2):
        add_product(lt_buf[:, pl.ds(256 * h2, 256)], e2, 8 * h2, 8)

    both = [ht[w2, 0, 4].astype(F32) + ht[w2, 1, 4].astype(F32) for w2 in range(8)]
    everything = both[0]
    for w2 in range(1, 8):
        everything = everything + both[w2]
    key = jnp.where(first, lane // 4, lane // 32)
    for b in range(16):
        t = jnp.where(first, everything, both[b // 2])
        mine = key == jnp.where(first, (b % 2) * 8 + b // 2, b % 2)
        t = jnp.sum(jnp.where(mine, t, 0.0), axis=1, keepdims=True)
        scale_buf[pl.ds(16 * b, 16), :] = jnp.broadcast_to(lax.rsqrt(t / D_ALL + 1e-06), (16, 128))
    own_scale = scale_buf[pl.ds(pl.multiple_of(16 * (2 * y + xl), 16), 16), pl.ds(0, 1)]

    scale = scale_buf[:, pl.ds(0, 1)]
    lt = jnp.concatenate([(acc[c] * scale).T for c in range(2)], axis=0)
    top = jnp.max(lt, axis=0, keepdims=True)
    lse = top + jnp.log(jnp.sum(jnp.exp(lt - top), axis=0, keepdims=True))
    lane4 = lax.broadcasted_iota(jnp.int32, (4, 128), 1)
    lane1 = lax.broadcasted_iota(jnp.int32, (1, 128), 1)
    ids4 = t_in[...]
    ids4 = jnp.where(first, ids4, pltpu.roll(ids4, 112, 1))
    half = jnp.zeros((4, 128), jnp.int32)
    for m in range(4):
        moved = ids4 if m == 0 else pltpu.roll(ids4, 128 - 16 * m, 1)
        half = jnp.where(lane4 // 16 == m, moved, half)
    far = pltpu.roll(half, 64, 1)
    own_ids = jnp.concatenate(
        [jnp.where(lane1 < 64, half[2 * r : 2 * r + 1], far[2 * r + 1 : 2 * r + 2]) for r in range(2)], axis=1
    )
    ids = lax.broadcasted_iota(jnp.int32, (2 * COLS, 256), 0) + (sec * 32 + tp - core) * COLS
    tgt = jnp.sum(jnp.where(ids == own_ids, lt, 0.0), axis=0, keepdims=True)

    def put(ref, lse, tgt):
        ref[0:1, :] = lse[:, 0:128]
        ref[1:2, :] = lse[:, 128:256]
        ref[2:3, :] = tgt[:, 0:128]
        ref[3:4, :] = tgt[:, 128:256]

    def merge(ref, n):
        ls = ref[:, 0:2, :]
        top = jnp.max(ls, axis=0)
        return top + jnp.log(jnp.sum(jnp.exp(ls - top[None]), axis=0)), jnp.sum(ref[:, 2:4, :], axis=0)

    put(st1.at[w], lse, tgt)

    def s1_copy(i):
        return send(st1.at[w], st1.at[w], s1_s.at[i], s1_r.at[i], line_dev(i))

    def s2_copy(i):
        return send(st2.at[x * 8 + u], st2.at[x * 8 + u], s2_s.at[i], s2_r.at[i], plane_dev(i))

    for i in (4, 3, 5, 2, 6, 1, 7):
        s1_copy(i).start()
    fh_out[...] = (m_buf[:, pl.ds(0, WID)] * own_scale * g_row).astype(BF16)
    lax.fori_loop(1, 8, waiter(s1_copy), 0)
    ls1, tg1 = merge(st1, 8)
    st2[x * 8 + u, 0:2, :] = ls1
    st2[x * 8 + u, 2:4, :] = tg1
    for du in (4, 3, 5, 2, 6, 1, 7, 0):
        for dx in (2, 1, 3, 0):
            if du or dx:
                s2_copy(8 * dx + du).start()
    lax.fori_loop(1, 32, waiter(s2_copy), 0)
    ls2, tg2 = merge(st2, 32)
    lp = tg2 - ls2
    turned = pltpu.roll(lp, 64, 1)
    rows4 = jnp.concatenate([lp[0:1], turned[0:1], lp[1:2], turned[1:2]], axis=0)
    wide = jnp.zeros((4, 128), F32)
    for m in range(4):
        moved = rows4 if m == 0 else pltpu.roll(rows4, 16 * m, 1)
        wide = jnp.where(lane4 // 16 == 2 * m, moved, wide)
    res[core] = jnp.where(first, wide, pltpu.roll(wide, 16, 1))
    c_res = send(res.at[core], res.at[core], core_s.at[4], core_r.at[4], sibling)
    c_res.start()

    c_pair.wait_send()
    for cp in c_emb:
        cp.wait_send()
    lax.fori_loop(1, 16, ender(rs_copy), 0)
    lax.fori_loop(1, 32, ender(wp_copy), 0)
    lax.fori_loop(1, 8, ender(xu_copy), 0)
    lax.fori_loop(1, 8, ender(xw_copy), 0)
    for k in (1, 2, 3):
        def x_end(z2, carry, k=k):
            x_copy(k, z2).wait_send()
            return carry
        lax.fori_loop(0, 8, x_end, 0)
    for cp in sent:
        cp.wait_send()
    lax.fori_loop(1, 8, ender(s1_copy), 0)
    lax.fori_loop(1, 32, ender(s2_copy), 0)
    c_res.wait()
    lp_out[...] = res[0] + res[1]


def hand_on(fh, lp, fh_out, lp_out):
    fh_out[...] = fh[...]
    lp_out[...] = lp[...]


def body(resid, act, w_down, gain, embed, targets):
    anyspec = pl.BlockSpec(memory_space=pl.ANY)
    vmem = pl.BlockSpec(memory_space=pltpu.VMEM)
    dma = pltpu.SemaphoreType.DMA
    fh, lp = pl.pallas_call(
        kernel,
        out_shape=(
            jax.ShapeDtypeStruct((16, WID), BF16),
            jax.ShapeDtypeStruct((4, 128), F32),
        ),
        in_specs=[anyspec] * 6,
        out_specs=(vmem, vmem),
        scratch_shapes=[
            pltpu.VMEM((2, 16, 16, HID), BF16),
            pltpu.VMEM((WID, HID), BF16),
            pltpu.VMEM((16, WID), BF16),
            pltpu.VMEM((WID,), F32),
            pltpu.VMEM((4, 128), jnp.int32),
            pltpu.VMEM((2, 16, 128, COLS), BF16),
            pltpu.VMEM((2, 16, 128, COLS), BF16),
            pltpu.VMEM((2, 16, 32, COLS), BF16),
            pltpu.VMEM((256, PADW), F32),
            pltpu.VMEM((256, PADW), F32),
            pltpu.VMEM((256, PADW), F32),
            pltpu.VMEM((16, 5, 8, 128), F32),
            pltpu.VMEM((16, 5, 8, 128), F32),
            pltpu.VMEM((16, PADW), F32),
            pltpu.VMEM((4, 64, 16, 128), BF16),
            pltpu.VMEM((8, 32, 16, 256), BF16),
            pltpu.VMEM((8, 2, 5, 16, 128), BF16),
            pltpu.VMEM((256, 512), BF16),
            pltpu.VMEM((256, 128), F32),
            pltpu.VMEM((2, 256, COLS), F32),
            pltpu.VMEM((8, 4, 128), F32),
            pltpu.VMEM((32, 4, 128), F32),
            pltpu.VMEM((2, 4, 128), F32),
            dma((9,)), dma((5,)), dma((5,)), dma((16,)), dma((16,)), dma((16,)), dma((16,)), dma((32,)), dma((32,)),
            dma((32,)), dma((32,)), dma((28,)), dma((28,)), dma((8,)), dma((8,)), dma((32,)), dma((32,)),
        ],
        compiler_params=pltpu.CompilerParams(
            collective_id=0, has_side_effects=True, vmem_limit_bytes=60 << 20
        ),
        name="ffn_vocab",
    )(
        act.reshape(16, 2, 16, HID),
        w_down.T,
        resid,
        gain,
        embed.reshape(16, WID, COLS),
        targets.reshape(4, 128),
    )
    fh, lp = pl.pallas_call(
        hand_on,
        out_shape=(
            jax.ShapeDtypeStruct((16, WID), BF16),
            jax.ShapeDtypeStruct((4, 128), F32),
        ),
        in_specs=[vmem] * 2,
        out_specs=(vmem, vmem),
        name="hand_on",
    )(fh, lp)
    return fh, lp.reshape(512)


def solution(mesh):
    return jax.shard_map(
        body,
        mesh=mesh,
        in_specs=(
            P("tp", "section"),
            P(None, "tp"),
            P("tp", "section"),
            P("section"),
            P(None, ("section", "tp")),
            P(),
        ),
        out_specs=(P("tp", "section"), P()),
        check_vma=False,
    )
```

```python
import jax
import jax.numpy as jnp
from jax import lax
from jax.experimental import pallas as pl
from jax.experimental.pallas import tpu as pltpu
from jax.sharding import PartitionSpec as P

MESH = pl.DeviceIdType.MESH
F32 = jnp.float32
BF16 = jnp.bfloat16
HID, WID = 1152, 288
D_ALL = 4608
PADW = 384
COLS = 256


def send(src, dst, s_sem, r_sem, dev):
    return pltpu.make_async_remote_copy(
        src_ref=src, dst_ref=dst, send_sem=s_sem, recv_sem=r_sem, device_id=dev, device_id_type=MESH
    )


def kernel(
    act, w_down, resid, gain, embed, targets,
    fh_out, lp_out,
    a_buf, w_buf, r_in, g_in, t_in, e0, e1, e2,
    p_out, p_in, p_own, s_buf, s_in, m_buf, hx, hw, ht, lt_buf, scale_buf, acc,
    st1, st2, res,
    ld_sem, core_s, core_r, rs_s, rs_r, xp_s, xp_r, wp_s, wp_r, xl_s, xl_r, wl_s, wl_r, s1_s, s1_r, s2_s, s2_r,
):
    sec = lax.axis_index("section")
    tp = lax.axis_index("tp")
    core = lax.rem(tp, 2)
    xl = lax.rem(tp // 2, 2)
    y = tp // 4
    xh = sec // 8
    z = lax.rem(sec, 8)
    x = 2 * xh + xl
    first = core == 0
    u = jnp.where(first, y, z)
    w = jnp.where(first, z, y)

    def dev(x2, y2, z2, c2):
        return ((x2 // 2) * 8 + z2, (y2 * 2 + lax.rem(x2, 2)) * 2 + c2)

    sibling = dev(x, y, z, 1 - core)

    def rs_peer(i):
        return lax.rem(y + i // 2, 8), lax.rem(xl + i, 2)

    def rs_dev(i):
        y2, xl2 = rs_peer(i)
        return dev(2 * xh + xl2, y2, z, core)

    def grid_dev(x2, u2, w2):
        return dev(x2, jnp.where(first, u2, w2), jnp.where(first, w2, u2), core)

    def plane_dev(i):
        return grid_dev(lax.rem(x + i // 8, 4), lax.rem(u + i, 8), w)

    def u_dev(i):
        return grid_dev(x, lax.rem(u + i, 8), w)

    def x_dev(k):
        return dev(2 * lax.rem(xh + k // 2, 2) + lax.rem(xl + k, 2), y, z, core)

    def line_dev(i):
        return grid_dev(x, u, lax.rem(w + i, 8))

    def load(src, dst, k):
        return pltpu.make_async_copy(src, dst, ld_sem.at[k])

    l_w = load(w_down, w_buf, 0)
    l_a0 = load(act.at[:, 1 - core], a_buf.at[0], 1)
    l_a1 = load(act.at[:, core], a_buf.at[1], 2)
    l_r = load(resid, r_in, 3)
    l_g = load(gain, g_in, 4)
    l_t = load(targets, t_in, 5)
    l_e = load(embed.at[:, pl.ds(0, 128)], e0.at[core], 6)
    l_f = load(embed.at[:, pl.ds(128, 128)], e1.at[core], 7)
    l_h = load(embed.at[:, pl.ds(256, 32)], e2.at[core], 8)
    for l in (l_w, l_a0, l_a1, l_r, l_g, l_t, l_e, l_f, l_h):
        l.start()

    barrier = pltpu.get_barrier_semaphore()
    pl.semaphore_signal(barrier, inc=1, device_id=sibling, device_id_type=MESH)

    def sig(peer):
        def go(i, carry):
            pl.semaphore_signal(barrier, inc=1, device_id=peer(i), device_id_type=MESH)
            return carry
        return go

    lax.fori_loop(0, 8, sig(lambda i: rs_dev(2 * i + 1)), 0)
    lax.fori_loop(1, 8, sig(line_dev), 0)
    lax.fori_loop(1, 32, sig(plane_dev), 0)

    p_out[:, pl.ds(256, 128)] = jnp.zeros((256, 128), F32)
    p_own[:, pl.ds(256, 128)] = jnp.zeros((256, 128), F32)

    def partial(k):
        return lax.dot_general(
            a_buf[k].reshape(256, HID), w_buf[...], (((1,), (1,)), ((), ())), preferred_element_type=F32
        )

    l_w.wait()
    l_a0.wait()
    p_out[:, pl.ds(0, WID)] = partial(0)
    pl.semaphore_wait(barrier, 1 + 8 + 7 + 31)
    c_pair = send(p_out, p_in, core_s.at[0], core_r.at[0], sibling)
    c_pair.start()
    l_a1.wait()
    p_own[:, pl.ds(0, WID)] = partial(1)
    c_pair.wait_recv()

    def pack(b):
        rows = pl.ds(pl.multiple_of(16 * b, 16), 16)
        v = p_own[rows, :] + p_in[rows, :]
        s_buf[b, 0] = v[0:8, 0:128]
        s_buf[b, 1] = v[0:8, 128:256]
        s_buf[b, 2] = v[8:16, 0:128]
        s_buf[b, 3] = v[8:16, 128:256]
        s_buf[b, 4] = v[0:8, 256:384] + pltpu.roll(v[8:16, 256:384], 32, 1)

    def rs_copy(i):
        y2, xl2 = rs_peer(i)
        return send(s_buf.at[y2 * 2 + xl2], s_in.at[i], rs_s.at[i], rs_r.at[i], rs_dev(i))

    def rs_start(i, carry):
        rs_copy(i).start()
        return carry

    for i in (8, 9, 6, 7, 10, 11, 4, 5, 12, 13, 2, 3, 14, 15, 1):
        y2, xl2 = rs_peer(i)
        pack(y2 * 2 + xl2)
        rs_copy(i).start()
    pack(y * 2 + xl)

    l_e.wait()
    l_f.wait()
    l_h.wait()
    c_emb = [
        send(e.at[core], e.at[core], core_s.at[k], core_r.at[k], sibling)
        for k, e in ((1, e0), (2, e1), (3, e2))
    ]
    for cp in c_emb:
        cp.start()
    l_r.wait()
    l_g.wait()
    l_t.wait()

    def rs_wait(i, carry):
        rs_copy(i).wait_recv()
        return carry

    lax.fori_loop(1, 16, rs_wait, 0)
    total = s_buf[y * 2 + xl]
    for i in range(1, 16):
        total = total + s_in[i]
    lane8 = lax.broadcasted_iota(jnp.int32, (8, 128), 1)
    m_buf[0:8, 0:128] = total[0]
    m_buf[0:8, 128:256] = total[1]
    m_buf[8:16, 0:128] = total[2]
    m_buf[8:16, 128:256] = total[3]
    m_buf[0:8, 256:384] = jnp.where(lane8 < 32, total[4], 0.0)
    m_buf[8:16, 256:384] = jnp.where(lane8 < 32, pltpu.roll(total[4], 96, 1), 0.0)
    g_row = g_in[...].reshape(1, WID)
    mixed = m_buf[:, pl.ds(0, WID)] + r_in[...].astype(F32)
    m_buf[:, pl.ds(0, WID)] = mixed
    sq = jnp.sum(mixed * mixed, axis=1, keepdims=True)
    sq_hi = sq.astype(BF16).astype(F32)
    sq_rest = sq - sq_hi
    sq_mid = sq_rest.astype(BF16).astype(F32)
    sq_lo = (sq_rest - sq_mid).astype(BF16).astype(F32)
    lane = lax.broadcasted_iota(jnp.int32, (16, 128), 1)
    tail = jnp.where(lane == 32, sq_hi, jnp.where(lane == 33, sq_mid, jnp.where(lane == 34, sq_lo, 0.0)))
    piece = (mixed * g_row).astype(BF16)
    w_own = hw.at[w, x * 8 + u]
    w_own[:, pl.ds(128, 128)] = tail.astype(BF16)
    w_own[:, pl.ds(0, 160)] = piece[:, 128:288]
    hx[x, w * 8 + u] = piece[:, 0:128]

    def starter(copy):
        def go(i, carry):
            copy(i).start()
            return carry
        return go

    def waiter(copy):
        def go(i, carry):
            copy(i).wait_recv()
            return carry
        return go

    def ender(copy):
        def go(i, carry):
            copy(i).wait_send()
            return carry
        return go

    def wp_copy(i):
        at = hw.at[w, x * 8 + u]
        return send(at, at, wp_s.at[i], wp_r.at[i], plane_dev(i))

    def xu_copy(i):
        at = hx.at[x, w * 8 + u]
        return send(at, at, xp_s.at[i], xp_r.at[i], u_dev(i))

    def chunk(w2):
        return hx.at[x, pl.ds(pl.multiple_of(w2 * 8, 8), 8)]

    def xw_copy(j):
        return send(chunk(w), chunk(w), xp_s.at[8 + j], xp_r.at[8 + j], line_dev(j))

    def x_copy(k, w2):
        return send(chunk(w2), chunk(w2), xl_s.at[k * 8 + w2], xl_r.at[k * 8 + w2], x_dev(k))

    def x_forward(j):
        xw_copy(j).wait_recv()
        for k in (2, 1, 3):
            x_copy(k, lax.rem(w + 8 - j, 8)).start()

    lax.fori_loop(1, 8, starter(xu_copy), 0)
    for du in (4, 3, 5, 2, 6, 1, 7, 0):
        for dx in (2, 1, 3, 0):
            if du or dx:
                wp_copy(8 * dx + du).start()
    lax.fori_loop(1, 8, waiter(xu_copy), 0)
    for j in (4, 3, 5, 2, 6, 1, 7):
        xw_copy(j).start()
    for k in (2, 1, 3):
        x_copy(k, w).start()
    lax.fori_loop(1, 32, waiter(wp_copy), 0)

    for c in range(2):
        squares = jnp.zeros((16, 128), F32)
        for j in range(4):
            tails = jnp.zeros((16, 128), F32)
            for i in range(4):
                q = 4 * j + i
                t = hw[w, 16 * c + q, :, pl.ds(128, 128)].astype(F32)
                tails = jnp.where(lane // 32 == i, pltpu.roll(t, 32 * i, 1) if i else t, tails)
                squares = jnp.where(
                    lane // 4 == q, pltpu.roll(t, (4 * q - 32) % 128, 1) if q != 8 else t, squares
                )
            ht[w, c, j] = tails.astype(BF16)
        ht[w, c, 4] = squares.astype(BF16)

    def w_copies(kind, c):
        step = (1, 7, 2, 6, 1, 7, 2, 6)[kind]
        at = lax.rem(w + (0, 0, 0, 0, 6, 2, 6, 2)[kind], 8)
        to = line_dev(step)
        slot_ = min(kind, 6) * 4 + c * 2
        main = hw.at[at, pl.ds(16 * c, 16), :, pl.ds(0, 128)]
        rest = ht.at[at, c]
        return [
            send(main, main, wl_s.at[slot_], wl_r.at[slot_], to),
            send(rest, rest, wl_s.at[slot_ + 1], wl_r.at[slot_ + 1], to),
        ]

    sent = []

    def w_send(kind, c):
        for cp in w_copies(kind, c):
            cp.start()
            sent.append(cp)

    def w_wait(kind, c):
        for cp in w_copies(kind, c):
            cp.wait_recv()

    for c in range(2):
        for kind in (2, 3, 0, 1):
            w_send(kind, c)

    for j in (1, 7, 2, 6, 3, 5, 4):
        x_forward(j)
    for c in range(2):
        for kind in (2, 3):
            w_wait(kind, c)
            w_send(kind + 2, c)
            if kind - 2 == c:
                w_send(kind + 4, c)

    acc[...] = jnp.zeros_like(acc)
    for cp in c_emb:
        cp.wait_recv()

    def slot(y2, x2, z2):
        return jnp.where(first, z2, y2), x2 * 8 + jnp.where(first, y2, z2)

    def place(y2, z2):
        return jnp.where(first, z2 * 8 + y2, y2 * 8 + z2)

    def add_product(lhs, e, s, n):
        for c in range(2):
            rhs = e[c, pl.ds(s, n)].reshape(256, COLS)
            acc[c] += jnp.dot(lhs, rhs, preferred_element_type=F32)

    def x_part(h2):
        def go(p, carry):
            cols = []
            for k in range(2):
                cols.append(
                    jnp.concatenate([hx[2 * h2 + b % 2, place(b // 2, 2 * p + k)] for b in range(16)], axis=0)
                )
            add_product(jnp.concatenate(cols, axis=1), e0, h2 * 8 + 2 * p, 2)
            return carry
        return go

    def w_part(h2):
        def go(p, carry):
            cols = []
            for k in range(2):
                tiles = []
                for b in range(16):
                    w2, p2 = slot(b // 2, 2 * h2 + b % 2, 2 * p + k)
                    tiles.append(hw[w2, p2, :, pl.ds(0, 128)])
                cols.append(jnp.concatenate(tiles, axis=0))
            add_product(jnp.concatenate(cols, axis=1), e1, h2 * 8 + 2 * p, 2)
            return carry
        return go

    def x_wait(k):
        def go(z2, carry):
            x_copy(k, z2).wait_recv()
            return carry
        lax.fori_loop(0, 8, go, 0)

    x_wait(1)
    lax.fori_loop(0, 4, x_part(xh), 0)
    x_wait(2)
    x_wait(3)
    lax.fori_loop(0, 4, x_part(1 - xh), 0)
    for c in range(2):
        for kind in (0, 1, 4, 5, 6):
            w_wait(kind, c)
        lax.fori_loop(0, 4, w_part(c), 0)

    @pl.when(first)
    def _():
        for h2 in range(2):
            for xl2 in range(2):
                for yq in range(2):
                    for zg in range(2):
                        src = [ht[4 * zg + i, h2, xl2 * 2 + yq].astype(F32) for i in range(4)]
                        for yi in range(4):
                            t = src[0]
                            for i in range(4):
                                by = 32 * ((i - yi) % 4)
                                moved = pltpu.roll(src[i], by, 1) if by else src[i]
                                t = jnp.where(lane // 32 == i, moved, t)
                            b = 2 * (4 * yq + yi) + xl2
                            lt_buf[pl.ds(16 * b, 16), pl.ds(128 * (2 * h2 + zg), 128)] = t.astype(BF16)

    @pl.when(jnp.logical_not(first))
    def _():
        for h2 in range(2):
            for b in range(16):
                for zg in range(2):
                    lt_buf[pl.ds(16 * b, 16), pl.ds(128 * (2 * h2 + zg), 128)] = ht[b // 2, h2, (b % 2) * 2 + zg]

    for h2 in range(2):
        add_product(lt_buf[:, pl.ds(256 * h2, 256)], e2, 8 * h2, 8)

    both = [ht[w2, 0, 4].astype(F32) + ht[w2, 1, 4].astype(F32) for w2 in range(8)]
    everything = both[0]
    for w2 in range(1, 8):
        everything = everything + both[w2]
    key = jnp.where(first, lane // 4, lane // 32)
    for b in range(16):
        t = jnp.where(first, everything, both[b // 2])
        mine = key == jnp.where(first, (b % 2) * 8 + b // 2, b % 2)
        t = jnp.sum(jnp.where(mine, t, 0.0), axis=1, keepdims=True)
        scale_buf[pl.ds(16 * b, 16), :] = jnp.broadcast_to(lax.rsqrt(t / D_ALL + 1e-06), (16, 128))
    own_scale = scale_buf[pl.ds(pl.multiple_of(16 * (2 * y + xl), 16), 16), pl.ds(0, 1)]

    scale = scale_buf[:, pl.ds(0, 1)]
    lt = jnp.concatenate([(acc[c] * scale).T for c in range(2)], axis=0)
    top = jnp.max(lt, axis=0, keepdims=True)
    lse = top + jnp.log(jnp.sum(jnp.exp(lt - top), axis=0, keepdims=True))
    lane4 = lax.broadcasted_iota(jnp.int32, (4, 128), 1)
    lane1 = lax.broadcasted_iota(jnp.int32, (1, 128), 1)
    ids4 = t_in[...]
    ids4 = jnp.where(first, ids4, pltpu.roll(ids4, 112, 1))
    half = jnp.zeros((4, 128), jnp.int32)
    for m in range(4):
        moved = ids4 if m == 0 else pltpu.roll(ids4, 128 - 16 * m, 1)
        half = jnp.where(lane4 // 16 == m, moved, half)
    far = pltpu.roll(half, 64, 1)
    own_ids = jnp.concatenate(
        [jnp.where(lane1 < 64, half[2 * r : 2 * r + 1], far[2 * r + 1 : 2 * r + 2]) for r in range(2)], axis=1
    )
    ids = lax.broadcasted_iota(jnp.int32, (2 * COLS, 256), 0) + (sec * 32 + tp - core) * COLS
    tgt = jnp.sum(jnp.where(ids == own_ids, lt, 0.0), axis=0, keepdims=True)

    def put(ref, lse, tgt):
        ref[0:1, :] = lse[:, 0:128]
        ref[1:2, :] = lse[:, 128:256]
        ref[2:3, :] = tgt[:, 0:128]
        ref[3:4, :] = tgt[:, 128:256]

    def merge(ref, n):
        ls = ref[:, 0:2, :]
        top = jnp.max(ls, axis=0)
        return top + jnp.log(jnp.sum(jnp.exp(ls - top[None]), axis=0)), jnp.sum(ref[:, 2:4, :], axis=0)

    put(st1.at[w], lse, tgt)

    def s1_copy(i):
        return send(st1.at[w], st1.at[w], s1_s.at[i], s1_r.at[i], line_dev(i))

    def s2_copy(i):
        return send(st2.at[x * 8 + u], st2.at[x * 8 + u], s2_s.at[i], s2_r.at[i], plane_dev(i))

    for i in (4, 3, 5, 2, 6, 1, 7):
        s1_copy(i).start()
    fh_out[...] = (m_buf[:, pl.ds(0, WID)] * own_scale * g_row).astype(BF16)
    lax.fori_loop(1, 8, waiter(s1_copy), 0)
    ls1, tg1 = merge(st1, 8)
    st2[x * 8 + u, 0:2, :] = ls1
    st2[x * 8 + u, 2:4, :] = tg1
    for du in (4, 3, 5, 2, 6, 1, 7, 0):
        for dx in (2, 1, 3, 0):
            if du or dx:
                s2_copy(8 * dx + du).start()
    lax.fori_loop(1, 32, waiter(s2_copy), 0)
    ls2, tg2 = merge(st2, 32)
    lp = tg2 - ls2
    turned = pltpu.roll(lp, 64, 1)
    rows4 = jnp.concatenate([lp[0:1], turned[0:1], lp[1:2], turned[1:2]], axis=0)
    wide = jnp.zeros((4, 128), F32)
    for m in range(4):
        moved = rows4 if m == 0 else pltpu.roll(rows4, 16 * m, 1)
        wide = jnp.where(lane4 // 16 == 2 * m, moved, wide)
    res[core] = jnp.where(first, wide, pltpu.roll(wide, 16, 1))
    c_res = send(res.at[core], res.at[core], core_s.at[4], core_r.at[4], sibling)
    c_res.start()

    c_pair.wait_send()
    for cp in c_emb:
        cp.wait_send()
    lax.fori_loop(1, 16, ender(rs_copy), 0)
    lax.fori_loop(1, 32, ender(wp_copy), 0)
    lax.fori_loop(1, 8, ender(xu_copy), 0)
    lax.fori_loop(1, 8, ender(xw_copy), 0)
    for k in (1, 2, 3):
        def x_end(z2, carry, k=k):
            x_copy(k, z2).wait_send()
            return carry
        lax.fori_loop(0, 8, x_end, 0)
    for cp in sent:
        cp.wait_send()
    lax.fori_loop(1, 8, ender(s1_copy), 0)
    lax.fori_loop(1, 32, ender(s2_copy), 0)
    c_res.wait()
    lp_out[...] = res[0] + res[1]


def hand_on(fh, lp, fh_out, lp_out):
    fh_out[...] = fh[...]
    lp_out[...] = lp[...]


def body(resid, act, w_down, gain, embed, targets):
    anyspec = pl.BlockSpec(memory_space=pl.ANY)
    vmem = pl.BlockSpec(memory_space=pltpu.VMEM)
    dma = pltpu.SemaphoreType.DMA
    fh, lp = pl.pallas_call(
        kernel,
        out_shape=(
            jax.ShapeDtypeStruct((16, WID), BF16),
            jax.ShapeDtypeStruct((4, 128), F32),
        ),
        in_specs=[anyspec] * 6,
        out_specs=(vmem, vmem),
        scratch_shapes=[
            pltpu.VMEM((2, 16, 16, HID), BF16),
            pltpu.VMEM((WID, HID), BF16),
            pltpu.VMEM((16, WID), BF16),
            pltpu.VMEM((WID,), F32),
            pltpu.VMEM((4, 128), jnp.int32),
            pltpu.VMEM((2, 16, 128, COLS), BF16),
            pltpu.VMEM((2, 16, 128, COLS), BF16),
            pltpu.VMEM((2, 16, 32, COLS), BF16),
            pltpu.VMEM((256, PADW), F32),
            pltpu.VMEM((256, PADW), F32),
            pltpu.VMEM((256, PADW), F32),
            pltpu.VMEM((16, 5, 8, 128), F32),
            pltpu.VMEM((16, 5, 8, 128), F32),
            pltpu.VMEM((16, PADW), F32),
            pltpu.VMEM((4, 64, 16, 128), BF16),
            pltpu.VMEM((8, 32, 16, 256), BF16),
            pltpu.VMEM((8, 2, 5, 16, 128), BF16),
            pltpu.VMEM((256, 512), BF16),
            pltpu.VMEM((256, 128), F32),
            pltpu.VMEM((2, 256, COLS), F32),
            pltpu.VMEM((8, 4, 128), F32),
            pltpu.VMEM((32, 4, 128), F32),
            pltpu.VMEM((2, 4, 128), F32),
            dma((9,)), dma((5,)), dma((5,)), dma((16,)), dma((16,)), dma((16,)), dma((16,)), dma((32,)), dma((32,)),
            dma((32,)), dma((32,)), dma((28,)), dma((28,)), dma((8,)), dma((8,)), dma((32,)), dma((32,)),
        ],
        compiler_params=pltpu.CompilerParams(
            collective_id=0, has_side_effects=True, vmem_limit_bytes=60 << 20
        ),
        name="ffn_vocab",
    )(
        act.reshape(16, 2, 16, HID),
        w_down.T,
        resid,
        gain,
        embed.reshape(16, WID, COLS),
        targets.reshape(4, 128),
    )
    fh, lp = pl.pallas_call(
        hand_on,
        out_shape=(
            jax.ShapeDtypeStruct((16, WID), BF16),
            jax.ShapeDtypeStruct((4, 128), F32),
        ),
        in_specs=[vmem] * 2,
        out_specs=(vmem, vmem),
        name="hand_on",
    )(fh, lp)
    return fh, lp.reshape(512)


def solution(mesh):
    return jax.shard_map(
        body,
        mesh=mesh,
        in_specs=(
            P("tp", "section"),
            P(None, "tp"),
            P("tp", "section"),
            P("section"),
            P(None, ("section", "tp")),
            P(),
        ),
        out_specs=(P("tp", "section"), P()),
        check_vma=False,
    )
```
